128 devices in a mesh: lat: 32 (over y, x, core), chan: 4 (over z).
Axes of the slice: x: 4, y: 4, z: 4, core: 2. Of those that a mesh axis runs over, the one named last changes fastest.
Arguments:
- grid_field: bfloat16 [512, 1440, 512], P('lat', None, 'chan'), may hold values from -6 to 6
- mode_lists: int32 [32, 16], replicated, may hold values from 0 to 511, as said below
- lat_basis: bfloat16 [512, 512, 512], P('lat'), may hold values from -0.25 to 0.25
- degree_gain: bfloat16 [512, 512], P(None, 'chan'), may hold values from 0.25 to 4
- channel_mixer: bfloat16 [2, 512, 512], P(None, 'chan'), may hold values from -0.1875 to 0.1875
Outputs:
- grid_out: bfloat16 [512, 1440, 512], P('lat', None, 'chan')
The draws below stay inside these ranges and needn't reach their ends.
Inputs may be any that keep to these rules, and one draw needn't show every extreme that they name: Every wavenumber of 0 to 511 stands exactly once in mode_lists; entries 2k and 2k + 1 of a row sum to 511.
All inputs are finite; a program needn't handle non-finite values.
Results may differ from the reference program's by a relative error of at most 0.01.
Values may be sent and summed in bfloat16 or wider, within the bound.
No kernel may reach another device: no remote copies, remote signals or barrier semaphores. Data moves between devices by JAX's collectives and lax.ppermute only.
A program may use at most 128 MiB of HBM per device.

```python
import math
import jax
import jax.numpy as jnp
from jax import lax

C = 512
NLON = 1440
MPD = 16
NLAT = 512
M = 512
L = 512
N_LAT = 32


def draw_mode_lists(key, part):
    key = jax.random.fold_in(key, 11)
    key_order, key_flip = jax.random.split(key)
    half_count = M // 2
    lower = jax.random.permutation(key_order, half_count).astype(jnp.int32)
    flips = jax.random.randint(key_flip, (half_count,), 0, 2).astype(jnp.int32)
    first = jnp.where(flips == 1, M - 1 - lower, lower)
    second = M - 1 - first
    paired = jnp.stack([first, second], axis=1)
    return paired.reshape(N_LAT, MPD).astype(jnp.int32)


def shard_levels(stream_key, extent, pieces, least, high):
    loudness = 1.0
    for dim, parts in pieces:
        draws = jax.random.uniform(jax.random.fold_in(jax.random.fold_in(stream_key, 6), dim), (parts,), jnp.float32, least / len(pieces), high / len(pieces))
        loudness = loudness * jnp.repeat(jnp.exp(draws), extent[dim] // parts).reshape((-1,) + (1,) * (len(extent) - 1 - dim))
    return loudness


def gaussian(rng, shape, deviation, limit, shards=(), kind=jnp.bfloat16):
    factor_of = shard_levels(rng, shape, shards, -0.22, 0.18) if shards else 1.0
    values = jax.random.normal(rng, shape, jnp.float32) * deviation * factor_of
    return jnp.minimum(jnp.maximum(values, -limit), limit).astype(kind)


def setup_inputs(seed: int = 0) -> dict:
    seeds = jax.random.split(jax.random.key(seed), 6)
    grid_field = gaussian(seeds[0], (NLAT, NLON, C), 1.0, 6.0, ((0, 32), (2, 4)))
    mode_lists = draw_mode_lists(jax.random.fold_in(seeds[5], 71), 0)
    lat_basis = gaussian(seeds[2], (M, L, NLAT), NLAT ** -0.5, 0.25, ((0, 32),))
    degree_gain = jnp.clip(jnp.exp(math.log(4.0) - 2.7725887 * jax.random.uniform(seeds[3], (L, C), jnp.float32) ** shard_levels(seeds[3], (L, C), ((1, 4),), -0.2, 0.2)), 0.25, 4.0).astype(jnp.bfloat16)
    channel_mixer = gaussian(seeds[4], (2, C, C), (2 * C) ** -0.5, 0.1875, ((1, 4),))
    return dict(grid_field=grid_field, mode_lists=mode_lists, lat_basis=lat_basis, degree_gain=degree_gain, channel_mixer=channel_mixer)


def longitude_table(wavenumbers, lon_count):
    longitudes = jnp.arange(lon_count, dtype=jnp.int32)
    phases = longitudes[:, None] * wavenumbers[None, :] % lon_count
    angles = phases.astype(jnp.float32) * (2.0 * math.pi / lon_count)
    factor = 1.0 / math.sqrt(lon_count)
    return jnp.stack([jnp.cos(angles) * factor, -jnp.sin(angles) * factor], axis=1).astype(jnp.bfloat16)

def complex_block(channel_mixer):
    real_part = channel_mixer[0]
    imag_part = channel_mixer[1]
    upper_rows = jnp.concatenate([real_part, imag_part], axis=1)
    bottom = jnp.concatenate([-imag_part, real_part], axis=1)
    return jnp.concatenate([upper_rows, bottom], axis=0)

def reference(grid_field, mode_lists, lat_basis, degree_gain, channel_mixer):
    wavenumbers = mode_lists.reshape(-1).astype(jnp.int32)
    flat_table = longitude_table(wavenumbers, NLON).reshape(NLON, 2 * M)

    def forward_row(lat_row):
        return jnp.dot(flat_table.T, lat_row, preferred_element_type=jnp.float32).astype(jnp.bfloat16)
    spectrum = lax.map(forward_row, grid_field).reshape(NLAT, 2, M, C)
    block_mix = complex_block(channel_mixer)
    gain_wide = jnp.tile(degree_gain.astype(jnp.float32), (1, 2))
    degrees = jnp.arange(L, dtype=jnp.int32)

    def per_slot(slot_index):
        wavenumber = wavenumbers[slot_index]
        basis_rows = jnp.where(degrees[:, None] >= wavenumber, lat_basis[slot_index], jnp.zeros((), jnp.bfloat16))
        column = lax.dynamic_index_in_dim(spectrum, slot_index, 2, keepdims=False).reshape(NLAT, 2 * C)
        coefficients = jnp.dot(basis_rows, column, preferred_element_type=jnp.float32)
        hidden = (coefficients * gain_wide).astype(jnp.bfloat16)
        mixed_out = jnp.dot(hidden, block_mix, preferred_element_type=jnp.float32).astype(jnp.bfloat16)
        return jnp.dot(basis_rows.T, mixed_out, preferred_element_type=jnp.float32).astype(jnp.bfloat16)
    returned = lax.map(per_slot, jnp.arange(M, dtype=jnp.int32))
    by_rows = returned.reshape(M, NLAT, 2, C).transpose(1, 2, 0, 3).reshape(NLAT, 2 * M, C)

    def inverse_row(lat_row):
        return jnp.dot(flat_table, lat_row, preferred_element_type=jnp.float32).astype(jnp.bfloat16)
    return lax.map(inverse_row, by_rows)
```

```python
import functools
import math

import jax
import jax.numpy as jnp
import ml_dtypes
import numpy as np
from jax import lax
from jax.experimental import pallas as pl
from jax.experimental.pallas import tpu as pltpu
from jax.sharding import PartitionSpec as P

BF16 = jnp.bfloat16
F32 = jnp.float32


def folded_tables(lon_count, wave_count):
    half = lon_count // 2
    waves = np.arange(wave_count).reshape(-1, 2).T
    phases = (waves[:, :, None] * np.arange(half)[None, None, :]) % lon_count
    angles = phases * (2.0 * math.pi / lon_count)
    factor = 1.0 / math.sqrt(lon_count)
    table = np.stack([np.cos(angles) * factor, -np.sin(angles) * factor], axis=2)
    table = table.reshape(2, wave_count, half).astype(np.float32).astype(ml_dtypes.bfloat16)
    return table, np.ascontiguousarray(table.transpose(0, 2, 1))


def fourier_kernel(modes, field, table, out, wide):
    step = pl.program_id(0)
    lats = field.shape[0]
    half = field.shape[1] // 2
    waves = table.shape[1]
    width = field.shape[2]
    band = out.shape[-2]
    low = jnp.concatenate([field[a, :half, :] for a in range(lats)], axis=1)
    high = jnp.concatenate([field[a, half:, :] for a in range(lats)], axis=1)
    for parity in range(2):
        folded = low + high if parity == 0 else low - high
        result = jnp.dot(table[parity], folded, preferred_element_type=F32)
        for a in range(lats):
            rows = pl.ds(parity * waves * band + step * lats + a, waves, stride=band)
            wide[rows, :] = result[:, a * width : (a + 1) * width]

    @pl.when(step == pl.num_programs(0) - 1)
    def _():
        def place(device, carry):
            for q in range(out.shape[1]):
                mode = modes[device * out.shape[1] + q]
                first = (mode % 2) * waves + (mode // 2) * 2
                for p in range(2):
                    start = pl.multiple_of((first + p) * band, band)
                    out[device, q, p] = wide[pl.ds(start, band), :].astype(BF16)
            return carry

        lax.fori_loop(0, out.shape[0], place, 0, unroll=4)


def fourier(modes, field, table, devices, slots):
    band, lon_count, width = field.shape
    waves = table.shape[1]
    lats = 2
    return pl.pallas_call(
        fourier_kernel,
        grid_spec=pltpu.PrefetchScalarGridSpec(
            num_scalar_prefetch=1,
            grid=(band // lats,),
            in_specs=[
                pl.BlockSpec((lats, lon_count, width), lambda i, m: (i, 0, 0)),
                pl.BlockSpec((2, waves, lon_count // 2), lambda i, m: (0, 0, 0)),
            ],
            out_specs=pl.BlockSpec(memory_space=pltpu.VMEM),
            scratch_shapes=[pltpu.VMEM((2 * waves * band, width), F32)],
        ),
        out_shape=jax.ShapeDtypeStruct((devices, slots, 2, band, width), BF16),
        compiler_params=pltpu.CompilerParams(vmem_limit_bytes=30 * 2**20),
        name="fourier",
    )(modes, field, table)


def inverse_kernel(modes, pieces, table, out, wide):
    step = pl.program_id(0)
    lats = out.shape[0]
    half = out.shape[1] // 2
    waves = table.shape[2]
    width = out.shape[2]
    band = pieces.shape[-2]

    @pl.when(step == 0)
    def _():
        def place(device, carry):
            for q in range(pieces.shape[1]):
                mode = modes[device * pieces.shape[1] + q]
                first = (mode % 2) * waves + (mode // 2) * 2
                for p in range(2):
                    start = pl.multiple_of((first + p) * band, band)
                    wide[pl.ds(start, band), :] = pieces[device, q, p].astype(F32)
            return carry

        lax.fori_loop(0, pieces.shape[0], place, 0, unroll=4)

    sums = []
    for parity in range(2):
        columns = []
        for a in range(lats):
            rows = pl.ds(parity * waves * band + step * lats + a, waves, stride=band)
            columns.append(wide[rows, :].astype(BF16))
        sums.append(
            jnp.dot(table[parity], jnp.concatenate(columns, axis=1), preferred_element_type=F32)
        )
    low = (sums[0] + sums[1]).astype(BF16)
    high = (sums[0] - sums[1]).astype(BF16)
    for a in range(lats):
        out[a, :half, :] = low[:, a * width : (a + 1) * width]
        out[a, half:, :] = high[:, a * width : (a + 1) * width]


def inverse(modes, pieces, table):
    devices, slots, _, band, width = pieces.shape
    _, half, waves = table.shape
    lats = 2
    return pl.pallas_call(
        inverse_kernel,
        grid_spec=pltpu.PrefetchScalarGridSpec(
            num_scalar_prefetch=1,
            grid=(band // lats,),
            in_specs=[
                pl.BlockSpec(memory_space=pltpu.VMEM),
                pl.BlockSpec((2, half, waves), lambda i, m: (0, 0, 0)),
            ],
            out_specs=pl.BlockSpec((lats, 2 * half, width), lambda i, m: (i, 0, 0)),
            scratch_shapes=[pltpu.VMEM((2 * waves * band, width), F32)],
        ),
        out_shape=jax.ShapeDtypeStruct((band, 2 * half, width), BF16),
        compiler_params=pltpu.CompilerParams(vmem_limit_bytes=30 * 2**20),
        name="inverse_fourier",
    )(modes, pieces, table)


def spectral_kernel(chosen, pieces, basis_low, basis_high, gain, mix, out, column, hidden, mixed):
    pair = pl.program_id(0)
    lat_parts, chan_parts, _, _, band, width = pieces.shape
    lat_count = lat_parts * band
    channels = chan_parts * width
    for which, basis in enumerate((basis_low, basis_high)):
        slot = chosen[pair, which]
        wave = chosen[pair, 2 + which]
        count = basis.shape[1]
        first = gain.shape[1] - count
        for p in range(2):
            for j in range(chan_parts):
                start = p * channels + j * width
                column[:, start : start + width] = pieces[:, j, slot, p].reshape(lat_count, width)
        degrees = first + lax.broadcasted_iota(jnp.int32, (count, lat_count), 0)
        kept = jnp.where(degrees >= wave, basis[0], jnp.zeros((), BF16))
        rows = 256
        for begin in range(0, count, rows):
            part = jnp.dot(kept[begin : begin + rows], column[...], preferred_element_type=F32)
            for p in range(2):
                for j in range(chan_parts):
                    start = p * channels + j * width
                    factor = gain[j, first + begin : first + begin + rows, :].astype(F32)
                    hidden[begin : begin + rows, start : start + width] = (
                        part[:, start : start + width] * factor
                    ).astype(BF16)
        for begin in range(0, count, rows):
            mixed[begin : begin + rows, :] = jnp.dot(
                hidden[begin : begin + rows, :], mix[...], preferred_element_type=F32
            ).astype(BF16)
        for p in range(2):
            for j in range(chan_parts):
                start = p * channels + j * width
                if j % 2:
                    continue
                back = lax.dot_general(
                    kept,
                    mixed[:count, start : start + 2 * width],
                    (((0,), (0,)), ((), ())),
                    preferred_element_type=F32,
                ).astype(BF16)
                for k in range(2):
                    out[:, j + k, slot, p] = back[:, k * width : (k + 1) * width].reshape(
                        lat_parts, band, width
                    )


def spectral(chosen, pieces, basis, gain, mix):
    lat_parts, chan_parts, slots, _, band, width = pieces.shape
    degrees, lat_count = basis.shape[1:]
    channels2 = mix.shape[0]
    return pl.pallas_call(
        spectral_kernel,
        grid_spec=pltpu.PrefetchScalarGridSpec(
            num_scalar_prefetch=1,
            grid=(slots // 2,),
            in_specs=[
                pl.BlockSpec(memory_space=pltpu.VMEM),
                pl.BlockSpec((1, degrees, lat_count), lambda i, c: (c[i, 4], 0, 0)),
                pl.BlockSpec((1, degrees // 2, lat_count), lambda i, c: (c[i, 5], 1, 0)),
                pl.BlockSpec(gain.shape, lambda i, c: (0, 0, 0)),
                pl.BlockSpec(mix.shape, lambda i, c: (0, 0)),
            ],
            out_specs=pl.BlockSpec(memory_space=pltpu.VMEM),
            scratch_shapes=[
                pltpu.VMEM((lat_count, channels2), BF16),
                pltpu.VMEM((degrees, channels2), BF16),
                pltpu.VMEM((degrees, channels2), BF16),
            ],
        ),
        out_shape=jax.ShapeDtypeStruct(pieces.shape, BF16),
        compiler_params=pltpu.CompilerParams(vmem_limit_bytes=36 * 2**20),
        name="spectral",
    )(chosen, pieces, basis, basis, gain, mix)


def pair_choice(mode_lists, lat_index, chan_index, slots):
    row = lax.dynamic_index_in_dim(mode_lists, lat_index, 0, keepdims=False)
    mine = lax.dynamic_slice_in_dim(row, chan_index * slots, slots).reshape(slots // 2, 2)
    swapped = (mine[:, 0] > mine[:, 1]).astype(jnp.int32)
    low_slot = 2 * jnp.arange(slots // 2, dtype=jnp.int32) + swapped
    high_slot = 2 * jnp.arange(slots // 2, dtype=jnp.int32) + 1 - swapped
    return jnp.stack(
        [
            low_slot,
            high_slot,
            jnp.minimum(mine[:, 0], mine[:, 1]),
            jnp.maximum(mine[:, 0], mine[:, 1]),
            low_slot + chan_index * slots,
            high_slot + chan_index * slots,
        ],
        axis=1,
    )


def local(lat_parts, chan_parts, grid_field, mode_lists, lat_basis, degree_gain, channel_mixer):
    devices = lat_parts * chan_parts
    slots = lat_basis.shape[0] // chan_parts
    width = grid_field.shape[2]
    channels = width * chan_parts
    forward_table, back_table = folded_tables(grid_field.shape[1], mode_lists.size)
    modes = mode_lists.reshape(-1)

    all_gain = lax.all_gather(degree_gain, "chan", axis=0)
    all_mixer = lax.all_gather(channel_mixer, "chan", axis=1, tiled=True)
    real, imag = all_mixer[0], all_mixer[1]
    mix = jnp.concatenate(
        [jnp.concatenate([real, imag], axis=1), jnp.concatenate([-imag, real], axis=1)], axis=0
    )
    chosen = pair_choice(mode_lists, lax.axis_index("lat"), lax.axis_index("chan"), slots)

    sent = fourier(modes, grid_field, jnp.asarray(forward_table), devices, slots)
    got = lax.all_to_all(sent, ("lat", "chan"), 0, 0, tiled=True)
    got = got.reshape((lat_parts, chan_parts) + got.shape[1:])
    back = spectral(chosen, got, lat_basis, all_gain, mix)
    back = back.reshape((devices,) + back.shape[2:])
    returned = lax.all_to_all(back, ("lat", "chan"), 0, 0, tiled=True)
    return inverse(modes, returned, jnp.asarray(back_table))


def solution(mesh):
    return jax.shard_map(
        functools.partial(local, mesh.shape["lat"], mesh.shape["chan"]),
        mesh=mesh,
        in_specs=(
            P("lat", None, "chan"),
            P(),
            P("lat", None, None),
            P(None, "chan"),
            P(None, "chan", None),
        ),
        out_specs=P("lat", None, "chan"),
        check_vma=False,
    )
```

```python
import functools
import math

import jax
import jax.numpy as jnp
import ml_dtypes
import numpy as np
from jax import lax
from jax.experimental import pallas as pl
from jax.experimental.pallas import tpu as pltpu
from jax.sharding import PartitionSpec as P

BF16 = jnp.bfloat16
F32 = jnp.float32
LATS = 4
SPACING = 24


def folded_tables(lon_count, wave_count):
    half = lon_count // 2
    waves = np.arange(wave_count).reshape(-1, 2).T
    phases = (waves[:, :, None] * np.arange(half)[None, None, :]) % lon_count
    angles = phases * (2.0 * math.pi / lon_count)
    factor = 1.0 / math.sqrt(lon_count)
    table = np.stack([np.cos(angles) * factor, -np.sin(angles) * factor], axis=2)
    table = table.reshape(2, wave_count, half).astype(np.float32).astype(ml_dtypes.bfloat16)
    return table, np.ascontiguousarray(table.transpose(0, 2, 1))


def for_each_tile(modes, devices, slots, move):
    per_row = modes.shape[0] // slots
    last = modes.shape[0] * modes.shape[1] - 1

    def row_step(row, carry):
        for pair in range(modes.shape[0] // 2):
            mode = modes[2 * pair, row]
            odd = mode & 1
            even_row = jnp.where(odd == 1, last - mode, mode) >> 1
            device = row * per_row + 2 * pair // slots
            first = 2 * pair % slots
            move(device, first + odd, 0, even_row)
            move(device, first + 1 - odd, 1, (last >> 1) - even_row)
        return carry

    lax.fori_loop(0, devices // per_row, row_step, 0)


def fourier_kernel(modes, field, table, out, even, odd):
    step = pl.program_id(0)
    lats, lon_count, width = field.shape
    half = lon_count // 2
    waves = table.shape[1]
    devices, slots, _, band, _ = out.shape
    wide = (even, odd)
    low = jnp.concatenate([field[a, :half, :] for a in range(lats)], axis=1)
    high = jnp.concatenate([field[a, half:, :] for a in range(lats)], axis=1)
    for parity in range(2):
        folded = low + high if parity == 0 else low - high
        result = jnp.dot(table[parity], folded, preferred_element_type=F32)
        for a in range(lats):
            rows = pl.ds(step * lats + a, waves, stride=SPACING)
            wide[parity][rows, :] = result[:, a * width : (a + 1) * width]

    def pack(device, slot, parity, row):
        for p in range(2):
            start = pl.multiple_of((2 * row + p) * SPACING, 8)
            out[device, slot, p] = wide[parity][pl.ds(start, band), :].astype(BF16)

    @pl.when(step == pl.num_programs(0) - 1)
    def _():
        for_each_tile(modes, devices, slots, pack)


def fourier(modes, field, table, devices, slots):
    band, lon_count, width = field.shape
    waves = table.shape[1]
    return pl.pallas_call(
        fourier_kernel,
        grid_spec=pltpu.PrefetchScalarGridSpec(
            num_scalar_prefetch=1,
            grid=(band // LATS,),
            in_specs=[
                pl.BlockSpec((LATS, lon_count, width), lambda i, m: (i, 0, 0)),
                pl.BlockSpec(table.shape, lambda i, m: (0, 0, 0)),
            ],
            out_specs=pl.BlockSpec(memory_space=pltpu.VMEM),
            scratch_shapes=[pltpu.VMEM((waves * SPACING, width), F32)] * 2,
        ),
        out_shape=jax.ShapeDtypeStruct((devices, slots, 2, band, width), BF16),
        compiler_params=pltpu.CompilerParams(vmem_limit_bytes=56 * 2**20),
        cost_estimate=pl.CostEstimate(
            flops=4 * band * lon_count * waves * width,
            bytes_accessed=2 * (band * lon_count * width + 4 * waves * band * width),
            transcendentals=0,
        ),
        name="fourier",
    )(modes, field, table)


def inverse_kernel(modes, pieces, table, out, even, odd):
    step = pl.program_id(0)
    lats, lon_count, width = out.shape
    half = lon_count // 2
    waves = table.shape[2]
    devices, slots, _, band, _ = pieces.shape
    wide = (even, odd)

    def unpack(device, slot, parity, row):
        for p in range(2):
            start = pl.multiple_of((2 * row + p) * SPACING, 8)
            wide[parity][pl.ds(start, band), :] = pieces[device, slot, p].astype(F32)

    @pl.when(step == 0)
    def _():
        for_each_tile(modes, devices, slots, unpack)

    sums = []
    for parity in range(2):
        columns = [
            wide[parity][pl.ds(step * lats + a, waves, stride=SPACING), :].astype(BF16)
            for a in range(lats)
        ]
        sums.append(
            jnp.dot(table[parity], jnp.concatenate(columns, axis=1), preferred_element_type=F32)
        )
    low = (sums[0] + sums[1]).astype(BF16)
    high = (sums[0] - sums[1]).astype(BF16)
    for a in range(lats):
        out[a, :half, :] = low[:, a * width : (a + 1) * width]
        out[a, half:, :] = high[:, a * width : (a + 1) * width]


def inverse(modes, pieces, table):
    devices, slots, _, band, width = pieces.shape
    _, half, waves = table.shape
    return pl.pallas_call(
        inverse_kernel,
        grid_spec=pltpu.PrefetchScalarGridSpec(
            num_scalar_prefetch=1,
            grid=(band // LATS,),
            in_specs=[
                pl.BlockSpec(memory_space=pltpu.VMEM),
                pl.BlockSpec(table.shape, lambda i, m: (0, 0, 0)),
            ],
            out_specs=pl.BlockSpec((LATS, 2 * half, width), lambda i, m: (i, 0, 0)),
            scratch_shapes=[pltpu.VMEM((waves * SPACING, width), F32)] * 2,
        ),
        out_shape=jax.ShapeDtypeStruct((band, 2 * half, width), BF16),
        compiler_params=pltpu.CompilerParams(vmem_limit_bytes=48 * 2**20),
        name="inverse_fourier",
    )(modes, pieces, table)


def spectral_kernel(
    modes, place, pieces, basis_low, basis_high, parts, out, mix, column, hidden, mixed
):
    pair = pl.program_id(0)
    lat_parts, chan_parts, slots, _, band, width = pieces.shape
    lat_count = lat_parts * band
    channels = chan_parts * width
    row, chan = place[0], place[1]
    from_chan = [(chan + chan_parts - hops) % chan_parts for hops in range(chan_parts)]

    @pl.when(pair == 0)
    def _():
        for hops in range(chan_parts):
            real, imag = parts[hops, :width, :], parts[hops, width : 2 * width, :]
            here, below = hops * width, channels + hops * width
            mix[here : here + width, :channels] = real
            mix[here : here + width, channels:] = imag
            mix[below : below + width, :channels] = -imag
            mix[below : below + width, channels:] = real

    first_mode = modes[chan * slots + 2 * pair, row]
    second_mode = modes[chan * slots + 2 * pair + 1, row]
    swapped = (first_mode > second_mode).astype(jnp.int32)
    for which, basis in enumerate((basis_low, basis_high)):
        slot = 2 * pair + (swapped if which == 0 else 1 - swapped)
        wave = jnp.minimum(first_mode, second_mode) if which == 0 else jnp.maximum(
            first_mode, second_mode
        )
        count = basis.shape[1]
        first = lat_count - count
        for p in range(2):
            for hops in range(chan_parts):
                start = p * channels + hops * width
                column[:, start : start + width] = pieces[:, from_chan[hops], slot, p].reshape(
                    lat_count, width
                )
        degrees = first + lax.broadcasted_iota(jnp.int32, (count, lat_count), 0)
        kept = jnp.where(degrees >= wave, basis[0], jnp.zeros((), BF16))
        rows = 256
        for begin in range(0, count, rows):
            part = jnp.dot(kept[begin : begin + rows], column[...], preferred_element_type=F32)
            for hops in range(chan_parts):
                for sub in range(0, rows, width):
                    degree = first + begin + sub
                    lane = degree // width * width
                    factor = parts[hops, 2 * width :, lane : lane + width].astype(F32)
                    for p in range(2):
                        start = p * channels + hops * width
                        hidden[begin + sub : begin + sub + width, start : start + width] = (
                            part[sub : sub + width, start : start + width] * factor
                        ).astype(BF16)
        for begin in range(0, count, rows):
            mixed[begin : begin + rows, :] = jnp.dot(
                hidden[begin : begin + rows, :], mix[...], preferred_element_type=F32
            ).astype(BF16)
        for p in range(2):
            for j in range(0, chan_parts, 2):
                start = p * channels + j * width
                back = lax.dot_general(
                    kept,
                    mixed[:count, start : start + 2 * width],
                    (((0,), (0,)), ((), ())),
                    preferred_element_type=F32,
                ).astype(BF16)
                for k in range(2):
                    out[:, j + k, slot, p] = back[:, k * width : (k + 1) * width].reshape(
                        lat_parts, band, width
                    )


def spectral(modes, place, pieces, basis, parts):
    lat_parts, chan_parts, slots, _, band, width = pieces.shape
    degrees, lat_count = basis.shape[1:]
    channels2 = 2 * chan_parts * width

    def basis_slot(which, pair, modes, place):
        begin = place[1] * slots + 2 * pair
        swapped = (modes[begin, place[0]] > modes[begin + 1, place[0]]).astype(jnp.int32)
        return begin + (swapped if which == 0 else 1 - swapped)

    return pl.pallas_call(
        spectral_kernel,
        grid_spec=pltpu.PrefetchScalarGridSpec(
            num_scalar_prefetch=2,
            grid=(slots // 2,),
            in_specs=[
                pl.BlockSpec(memory_space=pltpu.VMEM),
                pl.BlockSpec((1, degrees, lat_count), lambda i, m, c: (basis_slot(0, i, m, c), 0, 0)),
                pl.BlockSpec(
                    (1, degrees // 2, lat_count), lambda i, m, c: (basis_slot(1, i, m, c), 1, 0)
                ),
                pl.BlockSpec(memory_space=pltpu.VMEM),
            ],
            out_specs=pl.BlockSpec(memory_space=pltpu.VMEM),
            scratch_shapes=[
                pltpu.VMEM((channels2, channels2), BF16),
                pltpu.VMEM((lat_count, channels2), BF16),
                pltpu.VMEM((degrees, channels2), BF16),
                pltpu.VMEM((degrees, channels2), BF16),
            ],
        ),
        out_shape=jax.ShapeDtypeStruct(pieces.shape, BF16),
        compiler_params=pltpu.CompilerParams(vmem_limit_bytes=40 * 2**20),
        name="spectral",
    )(modes, place, pieces, basis, basis, parts)


def local(lat_parts, chan_parts, grid_field, mode_lists, lat_basis, degree_gain, channel_mixer):
    devices = lat_parts * chan_parts
    slots = lat_basis.shape[0] // chan_parts
    width = grid_field.shape[2]
    forward_table, back_table = folded_tables(grid_field.shape[1], mode_lists.size)
    modes = mode_lists.T

    mixer_rows = channel_mixer.reshape(2 * width, -1)
    gain_rows = degree_gain.reshape(-1, width, width)
    payload = jnp.concatenate(
        [mixer_rows, jnp.concatenate(list(gain_rows), axis=1)], axis=0
    )
    parts = [payload] + [
        lax.ppermute(payload, "chan", [(i, (i + hops) % chan_parts) for i in range(chan_parts)])
        for hops in range(1, chan_parts)
    ]
    place = jnp.stack([lax.axis_index("lat"), lax.axis_index("chan")]).astype(jnp.int32)

    sent = fourier(modes, grid_field, jnp.asarray(forward_table), devices, slots)
    sent, parts = lax.optimization_barrier((sent, parts))
    got = lax.all_to_all(sent, ("lat", "chan"), 0, 0, tiled=True)
    got = got.reshape((lat_parts, chan_parts) + got.shape[1:])
    back = spectral(modes, place, got, lat_basis, jnp.stack(parts))
    back = back.reshape((devices,) + back.shape[2:])
    returned = lax.all_to_all(back, ("lat", "chan"), 0, 0, tiled=True)
    return inverse(modes, returned, jnp.asarray(back_table))


def solution(mesh):
    return jax.shard_map(
        functools.partial(local, mesh.shape["lat"], mesh.shape["chan"]),
        mesh=mesh,
        in_specs=(
            P("lat", None, "chan"),
            P(),
            P("lat", None, None),
            P(None, "chan"),
            P(None, "chan", None),
        ),
        out_specs=P("lat", None, "chan"),
        check_vma=False,
    )
```

```python
import functools
import math

import jax
import jax.numpy as jnp
import ml_dtypes
import numpy as np
from jax import lax
from jax.experimental import pallas as pl
from jax.experimental.pallas import tpu as pltpu
from jax.sharding import PartitionSpec as P

BF16 = jnp.bfloat16
F32 = jnp.float32
LATS = 4
SPACING = 24


def folded_tables(lon_count, wave_count):
    half = lon_count // 2
    waves = np.arange(wave_count).reshape(-1, 2).T
    phases = (waves[:, :, None] * np.arange(half)[None, None, :]) % lon_count
    angles = phases * (2.0 * math.pi / lon_count)
    factor = 1.0 / math.sqrt(lon_count)
    table = np.stack([np.cos(angles) * factor, -np.sin(angles) * factor], axis=2)
    table = table.reshape(2, wave_count, half).astype(np.float32).astype(ml_dtypes.bfloat16)
    return table, np.ascontiguousarray(table.transpose(0, 2, 1))


def for_each_tile(modes, devices, slots, parities, move):
    per_row = modes.shape[0] // slots
    last = modes.shape[0] * modes.shape[1] - 1

    def row_step(row, carry):
        for pair in range(modes.shape[0] // 2):
            mode = modes[2 * pair, row]
            even_row = jnp.where(mode & 1 == 1, last - mode, mode) >> 1
            device = row * per_row + 2 * pair // slots
            for parity in parities:
                move(
                    device,
                    2 * pair % slots // 2,
                    parity,
                    even_row if parity == 0 else (last >> 1) - even_row,
                )
        return carry

    lax.fori_loop(0, devices // per_row, row_step, 0)


def fourier_kernel(parity, modes, field, table, *rest):
    out, wide = rest[-2:]
    step = pl.program_id(0)
    lats, lon_count, width = field.shape
    half = lon_count // 2
    waves = table.shape[1]
    devices = out.shape[0]
    pairs, _, band, _ = out.shape[-4:]
    low = jnp.concatenate([field[a, :half, :] for a in range(lats)], axis=1)
    high = jnp.concatenate([field[a, half:, :] for a in range(lats)], axis=1)
    folded = low + high if parity == 0 else low - high
    result = jnp.dot(table[0], folded, preferred_element_type=F32)
    for a in range(lats):
        rows = pl.ds(step * lats + a, waves, stride=SPACING)
        wide[rows, :] = result[:, a * width : (a + 1) * width]

    def pack(device, pair, parity, row):
        for p in range(2):
            start = pl.multiple_of((2 * row + p) * SPACING, 8)
            tile = wide[pl.ds(start, band), :].astype(BF16)
            if parity == 0:
                out[device, pair, p] = tile
            else:
                out[device, 1, pair, p] = tile

    @pl.when(step == pl.num_programs(0) - 1)
    def _():
        for_each_tile(modes, devices, 2 * pairs, (parity,), pack)

    if parity == 1:
        count = devices // (band // lats)
        rows = pl.ds(pl.multiple_of(step * count, count), count)
        out[rows, 0] = rest[0][rows]


def fourier(parity, modes, field, table, devices, slots, sent=None):
    band, lon_count, width = field.shape
    waves = table.shape[1]
    given = [] if sent is None else [sent]
    return pl.pallas_call(
        functools.partial(fourier_kernel, parity),
        grid_spec=pltpu.PrefetchScalarGridSpec(
            num_scalar_prefetch=1,
            grid=(band // LATS,),
            in_specs=[
                pl.BlockSpec((LATS, lon_count, width), lambda i, m: (i, 0, 0)),
                pl.BlockSpec((1,) + table.shape[1:], lambda i, m: (parity, 0, 0)),
            ]
            + [pl.BlockSpec(memory_space=pltpu.VMEM)] * len(given),
            out_specs=pl.BlockSpec(memory_space=pltpu.VMEM),
            scratch_shapes=[pltpu.VMEM((waves * SPACING, width), F32)],
        ),
        out_shape=jax.ShapeDtypeStruct(
            (devices,) + (2,) * len(given) + (slots // 2, 2, band, width), BF16
        ),
        compiler_params=pltpu.CompilerParams(vmem_limit_bytes=46 * 2**20),
        cost_estimate=pl.CostEstimate(
            flops=4 * band * lon_count * waves * width,
            bytes_accessed=2 * (band * lon_count * width + 4 * waves * band * width),
            transcendentals=0,
        ),
        name="fourier_odd" if parity else "fourier_even",
    )(modes, field, table, *given)


def inverse_kernel(modes, pieces, table, out, even, odd):
    step = pl.program_id(0)
    lats, lon_count, width = out.shape
    half = lon_count // 2
    waves = table.shape[2]
    devices, _, pairs, _, band, _ = pieces.shape
    wide = (even, odd)

    def unpack(device, pair, parity, row):
        for p in range(2):
            start = pl.multiple_of((2 * row + p) * SPACING, 8)
            wide[parity][pl.ds(start, band), :] = pieces[device, parity, pair, p].astype(F32)

    @pl.when(step == 0)
    def _():
        for_each_tile(modes, devices, 2 * pairs, (0, 1), unpack)

    sums = []
    for parity in range(2):
        columns = [
            wide[parity][pl.ds(step * lats + a, waves, stride=SPACING), :].astype(BF16)
            for a in range(lats)
        ]
        sums.append(
            jnp.dot(table[parity], jnp.concatenate(columns, axis=1), preferred_element_type=F32)
        )
    low = (sums[0] + sums[1]).astype(BF16)
    high = (sums[0] - sums[1]).astype(BF16)
    for a in range(lats):
        out[a, :half, :] = low[:, a * width : (a + 1) * width]
        out[a, half:, :] = high[:, a * width : (a + 1) * width]


def inverse(modes, pieces, table):
    band, width = pieces.shape[-2:]
    _, half, waves = table.shape
    return pl.pallas_call(
        inverse_kernel,
        grid_spec=pltpu.PrefetchScalarGridSpec(
            num_scalar_prefetch=1,
            grid=(band // LATS,),
            in_specs=[
                pl.BlockSpec(memory_space=pltpu.VMEM),
                pl.BlockSpec(table.shape, lambda i, m: (0, 0, 0)),
            ],
            out_specs=pl.BlockSpec((LATS, 2 * half, width), lambda i, m: (i, 0, 0)),
            scratch_shapes=[pltpu.VMEM((waves * SPACING, width), F32)] * 2,
        ),
        out_shape=jax.ShapeDtypeStruct((band, 2 * half, width), BF16),
        compiler_params=pltpu.CompilerParams(vmem_limit_bytes=48 * 2**20),
        name="inverse_fourier",
    )(modes, pieces, table)


def carry_kernel(place, mixer, gain, out):
    core = place[2]
    rows, width = mixer.shape[1], gain.shape[1]
    out[:rows, :] = mixer[core]
    blocks = out.shape[1] // width
    deep = gain.shape[0] // 2 // blocks
    for block in range(blocks):
        start = pl.multiple_of(core * (gain.shape[0] // 2) + block * deep, deep)
        out[rows:, block * width : (block + 1) * width] = gain[pl.ds(start, deep), :]


def carry(place, mixer, gain):
    rows = mixer.shape[1] + gain.size // 2 // mixer.shape[2]
    return pl.pallas_call(
        carry_kernel,
        in_specs=[pl.BlockSpec(memory_space=pltpu.SMEM)]
        + [pl.BlockSpec(memory_space=pltpu.VMEM)] * 2,
        out_specs=pl.BlockSpec(memory_space=pltpu.VMEM),
        out_shape=jax.ShapeDtypeStruct((rows, mixer.shape[2]), BF16),
        name="carry",
    )(place, mixer, gain)


def spectral_kernel(modes, place, pieces, basis_low, basis_high, mixer, gain, *rest):
    out, mix, gains, column, hidden, mixed = rest[-6:]
    pair = pl.program_id(0)
    lat_parts, chan_parts, _, pairs, _, band, width = pieces.shape
    shares = rest[: chan_parts - 1], rest[chan_parts - 1 : 2 * (chan_parts - 1)]
    lat_count = lat_parts * band
    channels = chan_parts * width
    row, chan, core = place[0], place[1], place[2]
    from_chan = [(chan + chan_parts - hops) % chan_parts for hops in range(chan_parts)]

    def place_mixer(hops, real, imag):
        here, below = hops * width, channels + hops * width
        if real is not None:
            mix[here : here + width, :channels] = real
            mix[below : below + width, channels:] = real
        if imag is not None:
            mix[here : here + width, channels:] = imag
            mix[below : below + width, :channels] = -imag

    def place_gain(hops, which, share):
        deep = share.shape[0] - width
        for block in range(chan_parts):
            start = pl.multiple_of(which * (gain.shape[0] // 2) + block * deep, deep)
            gains[hops, pl.ds(start, deep), :] = share[
                width:, block * width : (block + 1) * width
            ]

    @pl.when(pair == 0)
    def _():
        place_mixer(0, mixer[0], mixer[1])
        gains[0] = gain[...]
        for hops in range(1, chan_parts):
            for swap in range(2):
                share = shares[swap][hops - 1]
                place_gain(hops, core ^ swap, share)

                @pl.when(core ^ swap == 0)
                def _():
                    place_mixer(hops, share[:width, :], None)

                @pl.when(core ^ swap == 1)
                def _():
                    place_mixer(hops, None, share[:width, :])

    begin_mode = chan * 2 * pairs + 2 * pair
    lower = jnp.minimum(modes[begin_mode, row], modes[begin_mode + 1, row])
    higher = jnp.maximum(modes[begin_mode, row], modes[begin_mode + 1, row])
    for wave, basis in ((lower, basis_low), (higher, basis_high)):
        parity = wave & 1
        count = basis.shape[1]
        first = lat_count - count
        for p in range(2):
            for hops in range(chan_parts):
                start = p * channels + hops * width
                column[:, start : start + width] = pieces[
                    :, from_chan[hops], parity, pair, p
                ].reshape(lat_count, width)
        degrees = first + lax.broadcasted_iota(jnp.int32, (count, lat_count), 0)
        kept = jnp.where(degrees >= wave, basis[0], jnp.zeros((), BF16))
        rows = 256
        for begin in range(0, count, rows):
            part = jnp.dot(kept[begin : begin + rows], column[...], preferred_element_type=F32)
            for hops in range(chan_parts):
                factor = gains[hops, first + begin : first + begin + rows, :].astype(F32)
                for p in range(2):
                    start = p * channels + hops * width
                    hidden[begin : begin + rows, start : start + width] = (
                        part[:, start : start + width] * factor
                    ).astype(BF16)
        for begin in range(0, count, rows):
            mixed[begin : begin + rows, :] = jnp.dot(
                hidden[begin : begin + rows, :], mix[...], preferred_element_type=F32
            ).astype(BF16)
        for p in range(2):
            for j in range(0, chan_parts, 2):
                start = p * channels + j * width
                back = lax.dot_general(
                    kept,
                    mixed[:count, start : start + 2 * width],
                    (((0,), (0,)), ((), ())),
                    preferred_element_type=F32,
                ).astype(BF16)
                for k in range(2):
                    out[:, j + k, parity, pair, p] = back[:, k * width : (k + 1) * width].reshape(
                        lat_parts, band, width
                    )


def spectral(modes, place, pieces, basis, mixer, gain, shares):
    _, chan_parts, _, pairs, _, _, width = pieces.shape
    degrees, lat_count = basis.shape[1:]
    channels2 = 2 * chan_parts * width

    def basis_slot(which, pair, modes, place):
        begin = place[1] * 2 * pairs + 2 * pair
        swapped = (modes[begin, place[0]] > modes[begin + 1, place[0]]).astype(jnp.int32)
        return begin + (swapped if which == 0 else 1 - swapped)

    whole = pl.BlockSpec(memory_space=pltpu.VMEM)
    return pl.pallas_call(
        spectral_kernel,
        grid_spec=pltpu.PrefetchScalarGridSpec(
            num_scalar_prefetch=2,
            grid=(pairs,),
            in_specs=[
                whole,
                pl.BlockSpec((1, degrees, lat_count), lambda i, m, c: (basis_slot(0, i, m, c), 0, 0)),
                pl.BlockSpec(
                    (1, degrees // 2, lat_count), lambda i, m, c: (basis_slot(1, i, m, c), 1, 0)
                ),
                whole,
                whole,
            ]
            + [whole] * len(shares),
            out_specs=whole,
            scratch_shapes=[
                pltpu.VMEM((channels2, channels2), BF16),
                pltpu.VMEM((chan_parts,) + gain.shape, BF16),
                pltpu.VMEM((lat_count, channels2), BF16),
                pltpu.VMEM((degrees, channels2), BF16),
                pltpu.VMEM((degrees, channels2), BF16),
            ],
        ),
        out_shape=jax.ShapeDtypeStruct(pieces.shape, BF16),
        compiler_params=pltpu.CompilerParams(vmem_limit_bytes=40 * 2**20),
        name="spectral",
    )(modes, place, pieces, basis, basis, mixer, gain, *shares)


def local(lat_parts, chan_parts, grid_field, mode_lists, lat_basis, degree_gain, channel_mixer):
    devices = lat_parts * chan_parts
    slots = lat_basis.shape[0] // chan_parts
    forward_table, back_table = folded_tables(grid_field.shape[1], mode_lists.size)
    forward_table = jnp.asarray(forward_table)
    modes = mode_lists.T
    lat_index = lax.axis_index("lat")
    place = jnp.stack([lat_index, lax.axis_index("chan"), lat_index % 2]).astype(jnp.int32)

    share = carry(place, channel_mixer, degree_gain)
    shares = [
        lax.ppermute(share, "chan", [(i, (i + hops) % chan_parts) for i in range(chan_parts)])
        for hops in range(1, chan_parts)
    ]
    sent = fourier(0, modes, grid_field, forward_table, devices, slots)
    sent, shares = lax.optimization_barrier((sent, shares))
    swapped = [lax.ppermute(s, "lat", [(i, i ^ 1) for i in range(lat_parts)]) for s in shares]
    sent = fourier(1, modes, grid_field, forward_table, devices, slots, sent)
    sent, swapped, place = lax.optimization_barrier((sent, swapped, place))
    got = lax.all_to_all(sent, ("lat", "chan"), 0, 0, tiled=True)
    got = got.reshape((lat_parts, chan_parts) + got.shape[1:])
    back = spectral(
        modes, place, got, lat_basis, channel_mixer, degree_gain, shares + swapped
    )
    back = back.reshape((devices,) + back.shape[2:])
    returned = lax.all_to_all(back, ("lat", "chan"), 0, 0, tiled=True)
    return inverse(modes, returned, jnp.asarray(back_table))


def solution(mesh):
    return jax.shard_map(
        functools.partial(local, mesh.shape["lat"], mesh.shape["chan"]),
        mesh=mesh,
        in_specs=(
            P("lat", None, "chan"),
            P(),
            P("lat", None, None),
            P(None, "chan"),
            P(None, "chan", None),
        ),
        out_specs=P("lat", None, "chan"),
        check_vma=False,
    )
```

```python
import functools
import math

import jax
import jax.numpy as jnp
import ml_dtypes
import numpy as np
from jax import lax
from jax.experimental import pallas as pl
from jax.experimental.pallas import tpu as pltpu
from jax.sharding import PartitionSpec as P

BF16 = jnp.bfloat16
F32 = jnp.float32
LATS = 4
SPACING = 24


def folded_tables(lon_count, wave_count):
    half = lon_count // 2
    waves = np.arange(wave_count).reshape(-1, 2).T
    phases = (waves[:, :, None] * np.arange(half)[None, None, :]) % lon_count
    angles = phases * (2.0 * math.pi / lon_count)
    factor = 1.0 / math.sqrt(lon_count)
    table = np.stack([np.cos(angles) * factor, -np.sin(angles) * factor], axis=2)
    table = table.reshape(2, wave_count, half).astype(np.float32).astype(ml_dtypes.bfloat16)
    return table, np.ascontiguousarray(table.transpose(0, 2, 1))


def for_each_tile(modes, devices, slots, move, after=None):
    per_row = modes.shape[0] // slots
    last = modes.shape[0] * modes.shape[1] - 1

    def row_step(row, carry):
        for pair in range(modes.shape[0] // 2):
            mode = modes[2 * pair, row]
            even_row = jnp.where(mode & 1 == 1, last - mode, mode) >> 1
            device = row * per_row + 2 * pair // slots
            place = 2 * pair % slots // 2
            move(device, place, 0, even_row)
            move(device, place, 1, (last >> 1) - even_row)
        if after is not None:
            after(pl.ds(pl.multiple_of(row * per_row, per_row), per_row))
        return carry

    lax.fori_loop(0, devices // per_row, row_step, 0)


def fourier_kernel(modes, field, table, out, even, odd, packed, sem):
    step = pl.program_id(0)
    lats, lon_count, width = field.shape
    half = lon_count // 2
    waves = table.shape[1]
    devices, _, pairs, _, band, _ = out.shape
    wide = (even, odd)
    low = jnp.concatenate([field[a, :half, :] for a in range(lats)], axis=1)
    high = jnp.concatenate([field[a, half:, :] for a in range(lats)], axis=1)
    for parity in range(2):
        folded = low + high if parity == 0 else low - high
        result = jnp.dot(table[parity], folded, preferred_element_type=F32)
        for a in range(lats):
            rows = pl.ds(step * lats + a, waves, stride=SPACING)
            wide[parity][rows, :] = result[:, a * width : (a + 1) * width]

    def pack(device, pair, parity, row):
        for p in range(2):
            start = pl.multiple_of((2 * row + p) * SPACING, 8)
            packed[device, parity, pair, p] = wide[parity][pl.ds(start, band), :].astype(BF16)

    def send(some):
        pltpu.make_async_copy(packed.at[some], out.at[some], sem).start()

    @pl.when(step == pl.num_programs(0) - 1)
    def _():
        for_each_tile(modes, devices, 2 * pairs, pack, send)
        pltpu.make_async_copy(packed, out, sem).wait()


def fourier(modes, field, table, devices, slots):
    band, lon_count, width = field.shape
    waves = table.shape[1]
    shape = (devices, 2, slots // 2, 2, band, width)
    return pl.pallas_call(
        fourier_kernel,
        grid_spec=pltpu.PrefetchScalarGridSpec(
            num_scalar_prefetch=1,
            grid=(band // LATS,),
            in_specs=[
                pl.BlockSpec((LATS, lon_count, width), lambda i, m: (i, 0, 0)),
                pl.BlockSpec(table.shape, lambda i, m: (0, 0, 0)),
            ],
            out_specs=pl.BlockSpec(memory_space=pl.ANY),
            scratch_shapes=[pltpu.VMEM((waves * SPACING, width), F32)] * 2
            + [pltpu.VMEM(shape, BF16), pltpu.SemaphoreType.DMA],
        ),
        out_shape=jax.ShapeDtypeStruct(shape, BF16),
        compiler_params=pltpu.CompilerParams(vmem_limit_bytes=56 * 2**20),
        cost_estimate=pl.CostEstimate(
            flops=4 * band * lon_count * waves * width,
            bytes_accessed=2 * (band * lon_count * width + 4 * waves * band * width),
            transcendentals=0,
        ),
        name="fourier",
    )(modes, field, table)


def inverse_kernel(modes, pieces, table, out, even, odd):
    step = pl.program_id(0)
    lats, lon_count, width = out.shape
    half = lon_count // 2
    waves = table.shape[2]
    devices, _, pairs, _, band, _ = pieces.shape
    wide = (even, odd)

    def unpack(device, pair, parity, row):
        for p in range(2):
            start = pl.multiple_of((2 * row + p) * SPACING, 8)
            wide[parity][pl.ds(start, band), :] = pieces[device, parity, pair, p].astype(F32)

    @pl.when(step == 0)
    def _():
        for_each_tile(modes, devices, 2 * pairs, unpack)

    sums = []
    for parity in range(2):
        columns = [
            wide[parity][pl.ds(step * lats + a, waves, stride=SPACING), :].astype(BF16)
            for a in range(lats)
        ]
        sums.append(
            jnp.dot(table[parity], jnp.concatenate(columns, axis=1), preferred_element_type=F32)
        )
    low = (sums[0] + sums[1]).astype(BF16)
    high = (sums[0] - sums[1]).astype(BF16)
    for a in range(lats):
        out[a, :half, :] = low[:, a * width : (a + 1) * width]
        out[a, half:, :] = high[:, a * width : (a + 1) * width]


def inverse(modes, pieces, table):
    band, width = pieces.shape[-2:]
    _, half, waves = table.shape
    return pl.pallas_call(
        inverse_kernel,
        grid_spec=pltpu.PrefetchScalarGridSpec(
            num_scalar_prefetch=1,
            grid=(band // LATS,),
            in_specs=[
                pl.BlockSpec(memory_space=pltpu.VMEM),
                pl.BlockSpec(table.shape, lambda i, m: (0, 0, 0)),
            ],
            out_specs=pl.BlockSpec((LATS, 2 * half, width), lambda i, m: (i, 0, 0)),
            scratch_shapes=[pltpu.VMEM((waves * SPACING, width), F32)] * 2,
        ),
        out_shape=jax.ShapeDtypeStruct((band, 2 * half, width), BF16),
        compiler_params=pltpu.CompilerParams(vmem_limit_bytes=48 * 2**20),
        name="inverse_fourier",
    )(modes, pieces, table)


def carry_kernel(mixer, gain, out):
    core = lax.axis_index("lat") & 1
    rows, width = mixer.shape[1], gain.shape[1]
    out[:rows, :] = mixer[core]
    blocks = out.shape[1] // width
    deep = gain.shape[0] // 2 // blocks
    for block in range(blocks):
        start = pl.multiple_of(core * (gain.shape[0] // 2) + block * deep, deep)
        out[rows:, block * width : (block + 1) * width] = gain[pl.ds(start, deep), :]


def carry(mixer, gain):
    rows = mixer.shape[1] + gain.size // 2 // mixer.shape[2]
    return pl.pallas_call(
        carry_kernel,
        in_specs=[pl.BlockSpec(memory_space=pltpu.VMEM)] * 2,
        out_specs=pl.BlockSpec(memory_space=pltpu.VMEM),
        out_shape=jax.ShapeDtypeStruct((rows, mixer.shape[2]), BF16),
        name="carry",
    )(mixer, gain)


def spectral_kernel(modes, place, pieces, basis_low, basis_high, mixer, gain, *rest):
    out, mix, gains, column, hidden, mixed = rest[-6:]
    pair = pl.program_id(0)
    lat_parts, chan_parts, _, _, _, band, width = pieces.shape
    pairs = pl.num_programs(0)
    shares = rest[: chan_parts - 1], rest[chan_parts - 1 : 2 * (chan_parts - 1)]
    lat_count = lat_parts * band
    channels = chan_parts * width
    row, chan, core = place[0], place[1], place[2]
    from_chan = [(chan + chan_parts - hops) % chan_parts for hops in range(chan_parts)]

    def place_mixer(hops, real, imag):
        here, below = hops * width, channels + hops * width
        if real is not None:
            mix[here : here + width, :channels] = real
            mix[below : below + width, channels:] = real
        if imag is not None:
            mix[here : here + width, channels:] = imag
            mix[below : below + width, :channels] = -imag

    def place_gain(hops, which, share):
        deep = share.shape[0] - width
        for block in range(chan_parts):
            start = pl.multiple_of(which * (gain.shape[0] // 2) + block * deep, deep)
            gains[hops, pl.ds(start, deep), :] = share[
                width:, block * width : (block + 1) * width
            ]

    @pl.when(pair == 0)
    def _():
        place_mixer(0, mixer[0], mixer[1])
        gains[0] = gain[...]
        for hops in range(1, chan_parts):
            for swap in range(2):
                share = shares[swap][hops - 1]
                place_gain(hops, core ^ swap, share)

                @pl.when(core ^ swap == 0)
                def _():
                    place_mixer(hops, share[:width, :], None)

                @pl.when(core ^ swap == 1)
                def _():
                    place_mixer(hops, None, share[:width, :])

    begin_mode = chan * 2 * pairs + 2 * pair
    lower = jnp.minimum(modes[begin_mode, row], modes[begin_mode + 1, row])
    higher = jnp.maximum(modes[begin_mode, row], modes[begin_mode + 1, row])
    for wave, basis in ((lower, basis_low), (higher, basis_high)):
        parity = wave & 1
        count = basis.shape[1]
        first = lat_count - count
        for p in range(2):
            for hops in range(chan_parts):
                start = p * channels + hops * width
                column[:, start : start + width] = pieces[
                    :, from_chan[hops], parity, 0, p
                ].reshape(lat_count, width)
        degrees = first + lax.broadcasted_iota(jnp.int32, (count, lat_count), 0)
        kept = jnp.where(degrees >= wave, basis[0], jnp.zeros((), BF16))
        rows = 256
        for begin in range(0, count, rows):
            part = jnp.dot(kept[begin : begin + rows], column[...], preferred_element_type=F32)
            for hops in range(chan_parts):
                factor = gains[hops, first + begin : first + begin + rows, :].astype(F32)
                for p in range(2):
                    start = p * channels + hops * width
                    hidden[begin : begin + rows, start : start + width] = (
                        part[:, start : start + width] * factor
                    ).astype(BF16)
        for begin in range(0, count, rows):
            mixed[begin : begin + rows, :] = jnp.dot(
                hidden[begin : begin + rows, :], mix[...], preferred_element_type=F32
            ).astype(BF16)
        for p in range(2):
            for j in range(0, chan_parts, 2):
                start = p * channels + j * width
                back = lax.dot_general(
                    kept,
                    mixed[:count, start : start + 2 * width],
                    (((0,), (0,)), ((), ())),
                    preferred_element_type=F32,
                ).astype(BF16)
                for k in range(2):
                    out[:, j + k, parity, 0, p] = back[:, k * width : (k + 1) * width].reshape(
                        lat_parts, band, width
                    )


def spectral(modes, place, pieces, basis, mixer, gain, shares):
    _, chan_parts, _, pairs, _, _, width = pieces.shape
    degrees, lat_count = basis.shape[1:]
    channels2 = 2 * chan_parts * width

    def basis_slot(which, pair, modes, place):
        begin = place[1] * 2 * pairs + 2 * pair
        swapped = (modes[begin, place[0]] > modes[begin + 1, place[0]]).astype(jnp.int32)
        return begin + (swapped if which == 0 else 1 - swapped)

    whole = pl.BlockSpec(memory_space=pltpu.VMEM)
    one_pair = pl.BlockSpec(
        pieces.shape[:3] + (1,) + pieces.shape[4:], lambda i, m, c: (0, 0, 0, i, 0, 0, 0)
    )
    return pl.pallas_call(
        spectral_kernel,
        grid_spec=pltpu.PrefetchScalarGridSpec(
            num_scalar_prefetch=2,
            grid=(pairs,),
            in_specs=[
                one_pair,
                pl.BlockSpec((1, degrees, lat_count), lambda i, m, c: (basis_slot(0, i, m, c), 0, 0)),
                pl.BlockSpec(
                    (1, degrees // 2, lat_count), lambda i, m, c: (basis_slot(1, i, m, c), 1, 0)
                ),
                whole,
                whole,
            ]
            + [whole] * len(shares),
            out_specs=one_pair,
            scratch_shapes=[
                pltpu.VMEM((channels2, channels2), BF16),
                pltpu.VMEM((chan_parts,) + gain.shape, BF16),
                pltpu.VMEM((lat_count, channels2), BF16),
                pltpu.VMEM((degrees, channels2), BF16),
                pltpu.VMEM((degrees, channels2), BF16),
            ],
        ),
        out_shape=jax.ShapeDtypeStruct(pieces.shape, BF16),
        compiler_params=pltpu.CompilerParams(vmem_limit_bytes=40 * 2**20),
        name="spectral",
    )(modes, place, pieces, basis, basis, mixer, gain, *shares)


def local(lat_parts, chan_parts, grid_field, mode_lists, lat_basis, degree_gain, channel_mixer):
    devices = lat_parts * chan_parts
    slots = lat_basis.shape[0] // chan_parts
    forward_table, back_table = folded_tables(grid_field.shape[1], mode_lists.size)
    forward_table = jnp.asarray(forward_table)
    modes = mode_lists.T
    lat_index = lax.axis_index("lat")
    place = jnp.stack([lat_index, lax.axis_index("chan"), lat_index % 2]).astype(jnp.int32)

    share = carry(channel_mixer, degree_gain)
    shares = [
        lax.ppermute(share, "chan", [(i, (i + hops) % chan_parts) for i in range(chan_parts)])
        for hops in range(1, chan_parts)
    ]
    sent = fourier(modes, grid_field, forward_table, devices, slots)
    sent, shares = lax.optimization_barrier((sent, shares))
    swapped = [lax.ppermute(s, "lat", [(i, i ^ 1) for i in range(lat_parts)]) for s in shares]
    got = lax.all_to_all(sent, ("lat", "chan"), 0, 0, tiled=True)
    got = got.reshape((lat_parts, chan_parts) + got.shape[1:])
    back = spectral(
        modes, place, got, lat_basis, channel_mixer, degree_gain, shares + swapped
    )
    back = back.reshape((devices,) + back.shape[2:])
    returned = lax.all_to_all(back, ("lat", "chan"), 0, 0, tiled=True)
    return inverse(modes, returned, jnp.asarray(back_table))


def solution(mesh):
    return jax.shard_map(
        functools.partial(local, mesh.shape["lat"], mesh.shape["chan"]),
        mesh=mesh,
        in_specs=(
            P("lat", None, "chan"),
            P(),
            P("lat", None, None),
            P(None, "chan"),
            P(None, "chan", None),
        ),
        out_specs=P("lat", None, "chan"),
        check_vma=False,
    )
```

```python
import functools
import math

import jax
import jax.numpy as jnp
import ml_dtypes
import numpy as np
from jax import lax
from jax.experimental import pallas as pl
from jax.experimental.pallas import tpu as pltpu
from jax.sharding import PartitionSpec as P

BF16 = jnp.bfloat16
F32 = jnp.float32
LATS = 4
SPACING = 24


def folded_tables(lon_count, wave_count):
    half = lon_count // 2
    waves = np.arange(wave_count).reshape(-1, 2).T
    phases = (waves[:, :, None] * np.arange(half)[None, None, :]) % lon_count
    angles = phases * (2.0 * math.pi / lon_count)
    factor = 1.0 / math.sqrt(lon_count)
    table = np.stack([np.cos(angles) * factor, -np.sin(angles) * factor], axis=2)
    table = table.reshape(2, wave_count, half).astype(np.float32).astype(ml_dtypes.bfloat16)
    return table, np.ascontiguousarray(table.transpose(0, 2, 1))


def for_each_tile(modes, devices, slots, move, after=None):
    per_row = modes.shape[0] // slots
    last = modes.shape[0] * modes.shape[1] - 1

    def row_step(row, carry):
        for pair in range(modes.shape[0] // 2):
            mode = modes[2 * pair, row]
            even_row = jnp.where(mode & 1 == 1, last - mode, mode) >> 1
            device = row * per_row + 2 * pair // slots
            place = 2 * pair % slots // 2
            move(device, place, 0, even_row)
            move(device, place, 1, (last >> 1) - even_row)
        if after is not None:
            after(pl.ds(pl.multiple_of(row * per_row, per_row), per_row))
        return carry

    lax.fori_loop(0, devices // per_row, row_step, 0)


def fourier_kernel(modes, field, table, out, even, odd, packed, sem):
    step = pl.program_id(0)
    lats, lon_count, width = field.shape
    half = lon_count // 2
    waves = table.shape[1]
    devices, _, pairs, _, band, _ = out.shape
    wide = (even, odd)
    low = jnp.concatenate([field[a, :half, :] for a in range(lats)], axis=1)
    high = jnp.concatenate([field[a, half:, :] for a in range(lats)], axis=1)
    for parity in range(2):
        folded = low + high if parity == 0 else low - high
        result = jnp.dot(table[parity], folded, preferred_element_type=F32)
        for a in range(lats):
            rows = pl.ds(step * lats + a, waves, stride=SPACING)
            wide[parity][rows, :] = result[:, a * width : (a + 1) * width]

    def pack(device, pair, parity, row):
        for p in range(2):
            start = pl.multiple_of((2 * row + p) * SPACING, 8)
            packed[device, parity, pair, p] = wide[parity][pl.ds(start, band), :].astype(BF16)

    def send(some):
        pltpu.make_async_copy(packed.at[some], out.at[some], sem).start()

    @pl.when(step == pl.num_programs(0) - 1)
    def _():
        for_each_tile(modes, devices, 2 * pairs, pack, send)
        pltpu.make_async_copy(packed, out, sem).wait()


def fourier(modes, field, table, devices, slots):
    band, lon_count, width = field.shape
    waves = table.shape[1]
    shape = (devices, 2, slots // 2, 2, band, width)
    return pl.pallas_call(
        fourier_kernel,
        grid_spec=pltpu.PrefetchScalarGridSpec(
            num_scalar_prefetch=1,
            grid=(band // LATS,),
            in_specs=[
                pl.BlockSpec((LATS, lon_count, width), lambda i, m: (i, 0, 0)),
                pl.BlockSpec(table.shape, lambda i, m: (0, 0, 0)),
            ],
            out_specs=pl.BlockSpec(memory_space=pl.ANY),
            scratch_shapes=[pltpu.VMEM((waves * SPACING, width), F32)] * 2
            + [pltpu.VMEM(shape, BF16), pltpu.SemaphoreType.DMA],
        ),
        out_shape=jax.ShapeDtypeStruct(shape, BF16),
        compiler_params=pltpu.CompilerParams(vmem_limit_bytes=56 * 2**20),
        cost_estimate=pl.CostEstimate(
            flops=4 * band * lon_count * waves * width,
            bytes_accessed=2 * (band * lon_count * width + 4 * waves * band * width),
            transcendentals=0,
        ),
        name="fourier",
    )(modes, field, table)


def inverse_kernel(modes, pieces, table, out, even, odd):
    step = pl.program_id(0)
    lats, lon_count, width = out.shape
    half = lon_count // 2
    waves = table.shape[2]
    devices, _, pairs, _, band, _ = pieces.shape
    wide = (even, odd)

    def unpack(device, pair, parity, row):
        for p in range(2):
            start = pl.multiple_of((2 * row + p) * SPACING, 8)
            wide[parity][pl.ds(start, band), :] = pieces[device, parity, pair, p].astype(F32)

    @pl.when(step == 0)
    def _():
        for_each_tile(modes, devices, 2 * pairs, unpack)

    sums = []
    for parity in range(2):
        columns = [
            wide[parity][pl.ds(step * lats + a, waves, stride=SPACING), :].astype(BF16)
            for a in range(lats)
        ]
        sums.append(
            jnp.dot(table[parity], jnp.concatenate(columns, axis=1), preferred_element_type=F32)
        )
    low = (sums[0] + sums[1]).astype(BF16)
    high = (sums[0] - sums[1]).astype(BF16)
    for a in range(lats):
        out[a, :half, :] = low[:, a * width : (a + 1) * width]
        out[a, half:, :] = high[:, a * width : (a + 1) * width]


def inverse(modes, pieces, table):
    band, width = pieces.shape[-2:]
    _, half, waves = table.shape
    return pl.pallas_call(
        inverse_kernel,
        grid_spec=pltpu.PrefetchScalarGridSpec(
            num_scalar_prefetch=1,
            grid=(band // LATS,),
            in_specs=[
                pl.BlockSpec(memory_space=pltpu.VMEM),
                pl.BlockSpec(table.shape, lambda i, m: (0, 0, 0)),
            ],
            out_specs=pl.BlockSpec((LATS, 2 * half, width), lambda i, m: (i, 0, 0)),
            scratch_shapes=[pltpu.VMEM((waves * SPACING, width), F32)] * 2,
        ),
        out_shape=jax.ShapeDtypeStruct((band, 2 * half, width), BF16),
        compiler_params=pltpu.CompilerParams(vmem_limit_bytes=48 * 2**20),
        name="inverse_fourier",
    )(modes, pieces, table)


def carry_kernel(mixer, gain, out):
    core = lax.axis_index("lat") & 1
    rows, width = mixer.shape[1], gain.shape[1]
    out[:rows, :] = mixer[core]
    blocks = out.shape[1] // width
    deep = gain.shape[0] // 2 // blocks
    for block in range(blocks):
        start = pl.multiple_of(core * (gain.shape[0] // 2) + block * deep, deep)
        out[rows:, block * width : (block + 1) * width] = gain[pl.ds(start, deep), :]


def carry(mixer, gain):
    rows = mixer.shape[1] + gain.size // 2 // mixer.shape[2]
    return pl.pallas_call(
        carry_kernel,
        in_specs=[pl.BlockSpec(memory_space=pltpu.VMEM)] * 2,
        out_specs=pl.BlockSpec(memory_space=pltpu.VMEM),
        out_shape=jax.ShapeDtypeStruct((rows, mixer.shape[2]), BF16),
        name="carry",
    )(mixer, gain)


def gather_kernel(mixer, gain, *rest):
    mix, gains = rest[-2:]
    width = gain.shape[1]
    chan_parts = gains.shape[0]
    channels = chan_parts * width
    core = lax.axis_index("lat") & 1
    shares = rest[: chan_parts - 1], rest[chan_parts - 1 : 2 * (chan_parts - 1)]

    def place_mixer(hops, real, imag):
        here, below = hops * width, channels + hops * width
        if real is not None:
            mix[here : here + width, :channels] = real
            mix[below : below + width, channels:] = real
        if imag is not None:
            mix[here : here + width, channels:] = imag
            mix[below : below + width, :channels] = -imag

    place_mixer(0, mixer[0], mixer[1])
    gains[0] = gain[...]
    for hops in range(1, chan_parts):
        for swap in range(2):
            share = shares[swap][hops - 1]
            deep = share.shape[0] - width
            for block in range(chan_parts):
                start = pl.multiple_of((core ^ swap) * (gain.shape[0] // 2) + block * deep, deep)
                gains[hops, pl.ds(start, deep), :] = share[
                    width:, block * width : (block + 1) * width
                ]

            @pl.when(core ^ swap == 0)
            def _():
                place_mixer(hops, share[:width, :], None)

            @pl.when(core ^ swap == 1)
            def _():
                place_mixer(hops, None, share[:width, :])


def gather(mixer, gain, shares, chan_parts):
    channels2 = 2 * mixer.shape[2]
    whole = pl.BlockSpec(memory_space=pltpu.VMEM)
    return pl.pallas_call(
        gather_kernel,
        in_specs=[whole] * (2 + len(shares)),
        out_specs=[whole] * 2,
        out_shape=[
            jax.ShapeDtypeStruct((channels2, channels2), BF16),
            jax.ShapeDtypeStruct((chan_parts,) + gain.shape, BF16),
        ],
        compiler_params=pltpu.CompilerParams(vmem_limit_bytes=16 * 2**20),
        name="gather",
    )(mixer, gain, *shares)


def spectral_kernel(
    modes, place, pieces, basis_low, basis_high, mix, gains, out, column, hidden, mixed, kept_low, kept_high
):
    pair = pl.program_id(0)
    pairs = pl.num_programs(0)
    lat_parts, chan_parts, _, _, _, band, width = pieces.shape
    lat_count = lat_parts * band
    channels = chan_parts * width
    degrees = basis_low.shape[1]
    block = degrees // 4
    row, chan = place[0], place[1]
    from_chan = [(chan + chan_parts - hops) % chan_parts for hops in range(chan_parts)]

    begin_mode = chan * 2 * pairs + 2 * pair
    lower = jnp.minimum(modes[begin_mode, row], modes[begin_mode + 1, row])
    higher = jnp.maximum(modes[begin_mode, row], modes[begin_mode + 1, row])

    def masked(basis, begin, count, wave):
        kept = begin + lax.broadcasted_iota(jnp.int32, (count, lat_count), 0) >= wave
        first = begin - (degrees - basis.shape[1])
        return jnp.where(kept, basis[0, first : first + count, :], jnp.zeros((), BF16))

    kept_low[...] = masked(basis_low, 0, degrees, lower)
    kept_high[:block, :] = masked(basis_high, degrees - block, block, higher)
    kept_high[block:, :] = masked(basis_high, degrees - 2 * block, block, higher)

    def load_column(wave):
        for p in range(2):
            for hops in range(chan_parts):
                start = p * channels + hops * width
                column[:, start : start + width] = pieces[
                    :, from_chan[hops], wave & 1, 0, p
                ].reshape(lat_count, width)

    def analyse(kept, begin, count, target, spans):
        for p in range(2):
            part = jnp.dot(
                kept[begin : begin + count, :],
                column[:, p * channels : (p + 1) * channels],
                preferred_element_type=F32,
            )
            for hops in range(chan_parts):
                start = p * channels + hops * width
                for offset, rows, degree in spans:
                    factor = gains[hops, degree : degree + rows, :].astype(F32)
                    hidden[target + offset : target + offset + rows, start : start + width] = (
                        part[offset : offset + rows, hops * width : (hops + 1) * width] * factor
                    ).astype(BF16)

    wide_low = lower < block
    load_column(lower)

    @pl.when(wide_low)
    def _():
        analyse(kept_low, 0, degrees, 0, [(0, degrees, 0)])
        mixed[degrees + block :, :] = jnp.zeros((block, 2 * channels), BF16)

    @pl.when(jnp.logical_not(wide_low))
    def _():
        analyse(kept_low, block, degrees - block, block, [(0, degrees - block, block)])
        mixed[:block, :] = jnp.zeros((block, 2 * channels), BF16)

    load_column(higher)

    @pl.when(wide_low)
    def _():
        analyse(kept_high, 0, block, degrees, [(0, block, degrees - block)])

    @pl.when(jnp.logical_not(wide_low))
    def _():
        analyse(
            kept_high,
            0,
            2 * block,
            degrees,
            [(0, block, degrees - block), (block, block, degrees - 2 * block)],
        )

    rows = pl.ds(pl.multiple_of(jnp.where(wide_low, 0, block), block), degrees + block)
    for p in range(2):
        columns = slice(p * channels, (p + 1) * channels)
        mixed[rows, columns] = jnp.dot(
            hidden[rows, :], mix[:, columns], preferred_element_type=F32
        ).astype(BF16)

    for wave, kept, begin in ((lower, kept_low, 0), (higher, kept_high, degrees)):
        for p in range(2):
            for j in range(0, chan_parts, 2):
                start = p * channels + j * width
                back = lax.dot_general(
                    kept[...],
                    mixed[begin : begin + kept.shape[0], start : start + 2 * width],
                    (((0,), (0,)), ((), ())),
                    preferred_element_type=F32,
                ).astype(BF16)
                for k in range(2):
                    out[:, j + k, wave & 1, pair, p] = back[:, k * width : (k + 1) * width].reshape(
                        lat_parts, band, width
                    )


def spectral(modes, place, pieces, basis, mix, gains):
    _, chan_parts, _, pairs, _, _, width = pieces.shape
    degrees, lat_count = basis.shape[1:]
    channels2 = 2 * chan_parts * width

    def basis_slot(which, pair, modes, place):
        begin = place[1] * 2 * pairs + 2 * pair
        swapped = (modes[begin, place[0]] > modes[begin + 1, place[0]]).astype(jnp.int32)
        return begin + (swapped if which == 0 else 1 - swapped)

    whole = pl.BlockSpec(memory_space=pltpu.VMEM)
    one_pair = pl.BlockSpec(
        pieces.shape[:3] + (1,) + pieces.shape[4:], lambda i, m, c: (0, 0, 0, i, 0, 0, 0)
    )
    return pl.pallas_call(
        spectral_kernel,
        grid_spec=pltpu.PrefetchScalarGridSpec(
            num_scalar_prefetch=2,
            grid=(pairs,),
            in_specs=[
                one_pair,
                pl.BlockSpec((1, degrees, lat_count), lambda i, m, c: (basis_slot(0, i, m, c), 0, 0)),
                pl.BlockSpec(
                    (1, degrees // 2, lat_count), lambda i, m, c: (basis_slot(1, i, m, c), 1, 0)
                ),
                whole,
                whole,
            ],
            out_specs=whole,
            scratch_shapes=[
                pltpu.VMEM((lat_count, channels2), BF16),
                pltpu.VMEM((degrees + degrees // 2, channels2), BF16),
                pltpu.VMEM((degrees + degrees // 2, channels2), BF16),
                pltpu.VMEM((degrees, lat_count), BF16),
                pltpu.VMEM((degrees // 2, lat_count), BF16),
            ],
        ),
        out_shape=jax.ShapeDtypeStruct(pieces.shape, BF16),
        compiler_params=pltpu.CompilerParams(vmem_limit_bytes=40 * 2**20),
        name="spectral",
    )(modes, place, pieces, basis, basis, mix, gains)


def local(lat_parts, chan_parts, grid_field, mode_lists, lat_basis, degree_gain, channel_mixer):
    devices = lat_parts * chan_parts
    slots = lat_basis.shape[0] // chan_parts
    forward_table, back_table = folded_tables(grid_field.shape[1], mode_lists.size)
    forward_table = jnp.asarray(forward_table)
    modes = mode_lists.T
    lat_index = lax.axis_index("lat")
    place = jnp.stack([lat_index, lax.axis_index("chan")]).astype(jnp.int32)

    share = carry(channel_mixer, degree_gain)
    shares = [
        lax.ppermute(share, "chan", [(i, (i + hops) % chan_parts) for i in range(chan_parts)])
        for hops in range(1, chan_parts)
    ]
    sent = fourier(modes, grid_field, forward_table, devices, slots)
    sent, shares = lax.optimization_barrier((sent, shares))
    swapped = [lax.ppermute(s, "lat", [(i, i ^ 1) for i in range(lat_parts)]) for s in shares]
    got = lax.all_to_all(sent, ("lat", "chan"), 0, 0, tiled=True)
    got = got.reshape((lat_parts, chan_parts) + got.shape[1:])
    mix, gains = gather(channel_mixer, degree_gain, shares + swapped, chan_parts)
    back = spectral(modes, place, got, lat_basis, mix, gains)
    back = back.reshape((devices,) + back.shape[2:])
    returned = lax.all_to_all(back, ("lat", "chan"), 0, 0, tiled=True)
    return inverse(modes, returned, jnp.asarray(back_table))


def solution(mesh):
    return jax.shard_map(
        functools.partial(local, mesh.shape["lat"], mesh.shape["chan"]),
        mesh=mesh,
        in_specs=(
            P("lat", None, "chan"),
            P(),
            P("lat", None, None),
            P(None, "chan"),
            P(None, "chan", None),
        ),
        out_specs=P("lat", None, "chan"),
        check_vma=False,
    )
```

```python
import functools
import math

import jax
import jax.numpy as jnp
import ml_dtypes
import numpy as np
from jax import lax
from jax.experimental import pallas as pl
from jax.experimental.pallas import tpu as pltpu
from jax.sharding import PartitionSpec as P

BF16 = jnp.bfloat16
F32 = jnp.float32
LATS = 4
SPACING = 24


def folded_tables(lon_count, wave_count):
    half = lon_count // 2
    waves = np.arange(wave_count).reshape(-1, 2).T
    phases = (waves[:, :, None] * np.arange(half)[None, None, :]) % lon_count
    angles = phases * (2.0 * math.pi / lon_count)
    factor = 1.0 / math.sqrt(lon_count)
    table = np.stack([np.cos(angles) * factor, -np.sin(angles) * factor], axis=2)
    table = table.reshape(2, wave_count, half).astype(np.float32).astype(ml_dtypes.bfloat16)
    return table, np.ascontiguousarray(table.transpose(0, 2, 1))


def for_each_tile(modes, devices, slots, move, after=None):
    per_row = modes.shape[0] // slots
    last = modes.shape[0] * modes.shape[1] - 1

    def row_step(row, carry):
        for pair in range(modes.shape[0] // 2):
            mode = modes[2 * pair, row]
            even_row = jnp.where(mode & 1 == 1, last - mode, mode) >> 1
            device = row * per_row + 2 * pair // slots
            place = 2 * pair % slots // 2
            move(device, place, 0, even_row)
            move(device, place, 1, (last >> 1) - even_row)
        if after is not None:
            after(pl.ds(pl.multiple_of(row * per_row, per_row), per_row))
        return carry

    lax.fori_loop(0, devices // per_row, row_step, 0)


def fourier_kernel(modes, field, table, out, even, odd, packed, sem):
    step = pl.program_id(0)
    lats, lon_count, width = field.shape
    half = lon_count // 2
    waves = table.shape[1]
    devices, _, pairs, _, band, _ = out.shape
    wide = (even, odd)
    low = jnp.concatenate([field[a, :half, :] for a in range(lats)], axis=1)
    high = jnp.concatenate([field[a, half:, :] for a in range(lats)], axis=1)
    for parity in range(2):
        folded = low + high if parity == 0 else low - high
        result = jnp.dot(table[parity], folded, preferred_element_type=F32)
        for a in range(lats):
            rows = pl.ds(step * lats + a, waves, stride=SPACING)
            wide[parity][rows, :] = result[:, a * width : (a + 1) * width]

    def pack(device, pair, parity, row):
        for p in range(2):
            start = pl.multiple_of((2 * row + p) * SPACING, 8)
            packed[device, parity, pair, p] = wide[parity][pl.ds(start, band), :].astype(BF16)

    def send(some):
        pltpu.make_async_copy(packed.at[some], out.at[some], sem).start()

    @pl.when(step == pl.num_programs(0) - 1)
    def _():
        for_each_tile(modes, devices, 2 * pairs, pack, send)
        pltpu.make_async_copy(packed, out, sem).wait()


def fourier(modes, field, table, devices, slots):
    band, lon_count, width = field.shape
    waves = table.shape[1]
    shape = (devices, 2, slots // 2, 2, band, width)
    return pl.pallas_call(
        fourier_kernel,
        grid_spec=pltpu.PrefetchScalarGridSpec(
            num_scalar_prefetch=1,
            grid=(band // LATS,),
            in_specs=[
                pl.BlockSpec((LATS, lon_count, width), lambda i, m: (i, 0, 0)),
                pl.BlockSpec(table.shape, lambda i, m: (0, 0, 0)),
            ],
            out_specs=pl.BlockSpec(memory_space=pl.ANY),
            scratch_shapes=[pltpu.VMEM((waves * SPACING, width), F32)] * 2
            + [pltpu.VMEM(shape, BF16), pltpu.SemaphoreType.DMA],
        ),
        out_shape=jax.ShapeDtypeStruct(shape, BF16),
        compiler_params=pltpu.CompilerParams(vmem_limit_bytes=56 * 2**20),
        cost_estimate=pl.CostEstimate(
            flops=4 * band * lon_count * waves * width,
            bytes_accessed=2 * (band * lon_count * width + 4 * waves * band * width),
            transcendentals=0,
        ),
        name="fourier",
    )(modes, field, table)


def inverse_kernel(modes, pieces, table, out, even, odd):
    step = pl.program_id(0)
    lats, lon_count, width = out.shape
    half = lon_count // 2
    waves = table.shape[2]
    devices, _, pairs, _, band, _ = pieces.shape
    wide = (even, odd)

    def unpack(device, pair, parity, row):
        for p in range(2):
            start = pl.multiple_of((2 * row + p) * SPACING, 8)
            wide[parity][pl.ds(start, band), :] = pieces[device, parity, pair, p].astype(F32)

    @pl.when(step == 0)
    def _():
        for_each_tile(modes, devices, 2 * pairs, unpack)

    sums = []
    for parity in range(2):
        columns = [
            wide[parity][pl.ds(step * lats + a, waves, stride=SPACING), :].astype(BF16)
            for a in range(lats)
        ]
        sums.append(
            jnp.dot(table[parity], jnp.concatenate(columns, axis=1), preferred_element_type=F32)
        )
    low = (sums[0] + sums[1]).astype(BF16)
    high = (sums[0] - sums[1]).astype(BF16)
    for a in range(lats):
        out[a, :half, :] = low[:, a * width : (a + 1) * width]
        out[a, half:, :] = high[:, a * width : (a + 1) * width]


def inverse(modes, pieces, table):
    band, width = pieces.shape[-2:]
    _, half, waves = table.shape
    return pl.pallas_call(
        inverse_kernel,
        grid_spec=pltpu.PrefetchScalarGridSpec(
            num_scalar_prefetch=1,
            grid=(band // LATS,),
            in_specs=[
                pl.BlockSpec(memory_space=pltpu.VMEM),
                pl.BlockSpec(table.shape, lambda i, m: (0, 0, 0)),
            ],
            out_specs=pl.BlockSpec((LATS, 2 * half, width), lambda i, m: (i, 0, 0)),
            scratch_shapes=[pltpu.VMEM((waves * SPACING, width), F32)] * 2,
        ),
        out_shape=jax.ShapeDtypeStruct((band, 2 * half, width), BF16),
        compiler_params=pltpu.CompilerParams(vmem_limit_bytes=48 * 2**20),
        name="inverse_fourier",
    )(modes, pieces, table)


def carry_kernel(mixer, gain, out):
    core = lax.axis_index("lat") & 1
    rows, width = mixer.shape[1], gain.shape[1]
    out[:rows, :] = mixer[core]
    blocks = out.shape[1] // width
    deep = gain.shape[0] // 2 // blocks
    for block in range(blocks):
        start = pl.multiple_of(core * (gain.shape[0] // 2) + block * deep, deep)
        out[rows:, block * width : (block + 1) * width] = gain[pl.ds(start, deep), :]


def carry(mixer, gain):
    rows = mixer.shape[1] + gain.size // 2 // mixer.shape[2]
    return pl.pallas_call(
        carry_kernel,
        in_specs=[pl.BlockSpec(memory_space=pltpu.VMEM)] * 2,
        out_specs=pl.BlockSpec(memory_space=pltpu.VMEM),
        out_shape=jax.ShapeDtypeStruct((rows, mixer.shape[2]), BF16),
        name="carry",
    )(mixer, gain)


def gather_kernel(mixer, gain, *rest):
    mix, gains = rest[-2:]
    width = gain.shape[1]
    chan_parts = gains.shape[0]
    channels = chan_parts * width
    core = lax.axis_index("lat") & 1
    shares = rest[: chan_parts - 1], rest[chan_parts - 1 : 2 * (chan_parts - 1)]

    def place_mixer(hops, real, imag):
        here, below = hops * width, channels + hops * width
        if real is not None:
            mix[here : here + width, :channels] = real
            mix[below : below + width, channels:] = real
        if imag is not None:
            mix[here : here + width, channels:] = imag
            mix[below : below + width, :channels] = -imag

    place_mixer(0, mixer[0], mixer[1])
    gains[0] = gain[...]
    for hops in range(1, chan_parts):
        for swap in range(2):
            share = shares[swap][hops - 1]
            deep = share.shape[0] - width
            for block in range(chan_parts):
                start = pl.multiple_of((core ^ swap) * (gain.shape[0] // 2) + block * deep, deep)
                gains[hops, pl.ds(start, deep), :] = share[
                    width:, block * width : (block + 1) * width
                ]

            @pl.when(core ^ swap == 0)
            def _():
                place_mixer(hops, share[:width, :], None)

            @pl.when(core ^ swap == 1)
            def _():
                place_mixer(hops, None, share[:width, :])


def gather(mixer, gain, shares, chan_parts):
    channels2 = 2 * mixer.shape[2]
    whole = pl.BlockSpec(memory_space=pltpu.VMEM)
    return pl.pallas_call(
        gather_kernel,
        in_specs=[whole] * (2 + len(shares)),
        out_specs=[whole] * 2,
        out_shape=[
            jax.ShapeDtypeStruct((channels2, channels2), BF16),
            jax.ShapeDtypeStruct((chan_parts,) + gain.shape, BF16),
        ],
        compiler_params=pltpu.CompilerParams(vmem_limit_bytes=16 * 2**20),
        name="gather",
    )(mixer, gain, *shares)


def spectral_kernel(
    modes, place, pieces, basis_low, basis_high, mix, gains, out, column, hidden, mixed, kept_low, kept_high
):
    pair = pl.program_id(0)
    pairs = pl.num_programs(0)
    lat_parts, chan_parts, _, _, _, band, width = pieces.shape
    lat_count = lat_parts * band
    channels = chan_parts * width
    degrees = basis_low.shape[1]
    block = degrees // 4
    row, chan = place[0], place[1]
    from_chan = [(chan + chan_parts - hops) % chan_parts for hops in range(chan_parts)]

    begin_mode = chan * 2 * pairs + 2 * pair
    lower = jnp.minimum(modes[begin_mode, row], modes[begin_mode + 1, row])
    higher = jnp.maximum(modes[begin_mode, row], modes[begin_mode + 1, row])

    def masked(basis, begin, count, wave):
        kept = begin + lax.broadcasted_iota(jnp.int32, (count, lat_count), 0) >= wave
        first = begin - (degrees - basis.shape[1])
        return jnp.where(kept, basis[0, first : first + count, :], jnp.zeros((), BF16))

    kept_low[...] = masked(basis_low, 0, degrees, lower)
    kept_high[:block, :] = masked(basis_high, degrees - block, block, higher)
    kept_high[block:, :] = masked(basis_high, degrees - 2 * block, block, higher)

    def load_column(wave):
        for p in range(2):
            for hops in range(chan_parts):
                start = p * channels + hops * width
                column[:, start : start + width] = pieces[
                    :, from_chan[hops], wave & 1, 0, p
                ].reshape(lat_count, width)

    def analyse(kept, begin, count, target, spans):
        for p in range(2):
            part = jnp.dot(
                kept[begin : begin + count, :],
                column[:, p * channels : (p + 1) * channels],
                preferred_element_type=F32,
            )
            for hops in range(chan_parts):
                start = p * channels + hops * width
                for offset, rows, degree in spans:
                    factor = gains[hops, degree : degree + rows, :].astype(F32)
                    hidden[target + offset : target + offset + rows, start : start + width] = (
                        part[offset : offset + rows, hops * width : (hops + 1) * width] * factor
                    ).astype(BF16)

    wide_low = lower < block
    load_column(lower)

    @pl.when(wide_low)
    def _():
        analyse(kept_low, 0, degrees, 0, [(0, degrees, 0)])
        mixed[degrees + block :, :] = jnp.zeros((block, 2 * channels), BF16)

    @pl.when(jnp.logical_not(wide_low))
    def _():
        analyse(kept_low, block, degrees - block, block, [(0, degrees - block, block)])
        mixed[:block, :] = jnp.zeros((block, 2 * channels), BF16)

    load_column(higher)

    @pl.when(wide_low)
    def _():
        analyse(kept_high, 0, block, degrees, [(0, block, degrees - block)])

    @pl.when(jnp.logical_not(wide_low))
    def _():
        analyse(
            kept_high,
            0,
            2 * block,
            degrees,
            [(0, block, degrees - block), (block, block, degrees - 2 * block)],
        )

    rows = pl.ds(pl.multiple_of(jnp.where(wide_low, 0, block), block), degrees + block)
    for p in range(2):
        columns = slice(p * channels, (p + 1) * channels)
        mixed[rows, columns] = jnp.dot(
            hidden[rows, :], mix[:, columns], preferred_element_type=F32
        ).astype(BF16)

    for wave, kept, begin in ((lower, kept_low, 0), (higher, kept_high, degrees)):
        for p in range(2):
            for j in range(0, chan_parts, 2):
                start = p * channels + j * width
                back = lax.dot_general(
                    kept[...],
                    mixed[begin : begin + kept.shape[0], start : start + 2 * width],
                    (((0,), (0,)), ((), ())),
                    preferred_element_type=F32,
                ).astype(BF16)
                for k in range(2):
                    out[:, j + k, wave & 1, pair, p] = back[:, k * width : (k + 1) * width].reshape(
                        lat_parts, band, width
                    )


def spectral(modes, place, pieces, basis, mix, gains):
    _, chan_parts, _, pairs, _, _, width = pieces.shape
    degrees, lat_count = basis.shape[1:]
    channels2 = 2 * chan_parts * width

    def basis_slot(which, pair, modes, place):
        begin = place[1] * 2 * pairs + 2 * pair
        swapped = (modes[begin, place[0]] > modes[begin + 1, place[0]]).astype(jnp.int32)
        return begin + (swapped if which == 0 else 1 - swapped)

    whole = pl.BlockSpec(memory_space=pltpu.VMEM)
    one_pair = pl.BlockSpec(
        pieces.shape[:3] + (1,) + pieces.shape[4:], lambda i, m, c: (0, 0, 0, i, 0, 0, 0)
    )
    return pl.pallas_call(
        spectral_kernel,
        grid_spec=pltpu.PrefetchScalarGridSpec(
            num_scalar_prefetch=2,
            grid=(pairs,),
            in_specs=[
                one_pair,
                pl.BlockSpec((1, degrees, lat_count), lambda i, m, c: (basis_slot(0, i, m, c), 0, 0)),
                pl.BlockSpec(
                    (1, degrees // 2, lat_count), lambda i, m, c: (basis_slot(1, i, m, c), 1, 0)
                ),
                whole,
                whole,
            ],
            out_specs=whole,
            scratch_shapes=[
                pltpu.VMEM((lat_count, channels2), BF16),
                pltpu.VMEM((degrees + degrees // 2, channels2), BF16),
                pltpu.VMEM((degrees + degrees // 2, channels2), BF16),
                pltpu.VMEM((degrees, lat_count), BF16),
                pltpu.VMEM((degrees // 2, lat_count), BF16),
            ],
        ),
        out_shape=jax.ShapeDtypeStruct(pieces.shape, BF16),
        compiler_params=pltpu.CompilerParams(vmem_limit_bytes=40 * 2**20),
        name="spectral",
    )(modes, place, pieces, basis, basis, mix, gains)


def local(lat_parts, chan_parts, grid_field, mode_lists, lat_basis, degree_gain, channel_mixer):
    devices = lat_parts * chan_parts
    slots = lat_basis.shape[0] // chan_parts
    forward_table, back_table = folded_tables(grid_field.shape[1], mode_lists.size)
    forward_table = jnp.asarray(forward_table)
    modes = mode_lists.T
    lat_index = lax.axis_index("lat")
    place = jnp.stack([lat_index, lax.axis_index("chan")]).astype(jnp.int32)

    share = carry(channel_mixer, degree_gain)
    shares = [
        lax.ppermute(share, "chan", [(i, (i + hops) % chan_parts) for i in range(chan_parts)])
        for hops in range(1, chan_parts)
    ]
    sent = fourier(modes, grid_field, forward_table, devices, slots)
    swapped = [lax.ppermute(s, "lat", [(i, i ^ 1) for i in range(lat_parts)]) for s in shares]
    got = lax.all_to_all(sent, ("lat", "chan"), 0, 0, tiled=True)
    got = got.reshape((lat_parts, chan_parts) + got.shape[1:])
    mix, gains = gather(channel_mixer, degree_gain, shares + swapped, chan_parts)
    back = spectral(modes, place, got, lat_basis, mix, gains)
    back = back.reshape((devices,) + back.shape[2:])
    returned = lax.all_to_all(back, ("lat", "chan"), 0, 0, tiled=True)
    return inverse(modes, returned, jnp.asarray(back_table))


def solution(mesh):
    return jax.shard_map(
        functools.partial(local, mesh.shape["lat"], mesh.shape["chan"]),
        mesh=mesh,
        in_specs=(
            P("lat", None, "chan"),
            P(),
            P("lat", None, None),
            P(None, "chan"),
            P(None, "chan", None),
        ),
        out_specs=P("lat", None, "chan"),
        check_vma=False,
    )
```

```python
import functools
import math

import jax
import jax.numpy as jnp
import ml_dtypes
import numpy as np
from jax import lax
from jax.experimental import pallas as pl
from jax.experimental.pallas import tpu as pltpu
from jax.sharding import PartitionSpec as P

BF16 = jnp.bfloat16
F32 = jnp.float32
LATS = 4
SPACING = 24


def folded_tables(lon_count, wave_count):
    half = lon_count // 2
    waves = np.arange(wave_count).reshape(-1, 2).T
    phases = (waves[:, :, None] * np.arange(half)[None, None, :]) % lon_count
    angles = phases * (2.0 * math.pi / lon_count)
    factor = 1.0 / math.sqrt(lon_count)
    table = np.stack([np.cos(angles) * factor, -np.sin(angles) * factor], axis=2)
    table = table.reshape(2, wave_count, half).astype(np.float32).astype(ml_dtypes.bfloat16)
    return table, np.ascontiguousarray(table.transpose(0, 2, 1))


def for_each_tile(modes, devices, slots, move, after=None):
    per_row = modes.shape[0] // slots
    last = modes.shape[0] * modes.shape[1] - 1

    def row_step(row, carry):
        for pair in range(modes.shape[0] // 2):
            mode = modes[2 * pair, row]
            even_row = jnp.where(mode & 1 == 1, last - mode, mode) >> 1
            device = row * per_row + 2 * pair // slots
            place = 2 * pair % slots // 2
            move(device, place, 0, even_row)
            move(device, place, 1, (last >> 1) - even_row)
        if after is not None:
            after(pl.ds(pl.multiple_of(row * per_row, per_row), per_row))
        return carry

    lax.fori_loop(0, devices // per_row, row_step, 0)


def fourier_kernel(modes, field, table, out, even, odd, packed, sem):
    step = pl.program_id(0)
    lats, lon_count, width = field.shape
    half = lon_count // 2
    waves = table.shape[1]
    devices, _, pairs, _, band, _ = out.shape
    wide = (even, odd)
    low = jnp.concatenate([field[a, :half, :] for a in range(lats)], axis=1)
    high = jnp.concatenate([field[a, half:, :] for a in range(lats)], axis=1)
    for parity in range(2):
        folded = low + high if parity == 0 else low - high
        result = jnp.dot(table[parity], folded, preferred_element_type=F32)
        for a in range(lats):
            rows = pl.ds(step * lats + a, waves, stride=SPACING)
            wide[parity][rows, :] = result[:, a * width : (a + 1) * width]

    def pack(device, pair, parity, row):
        for p in range(2):
            start = pl.multiple_of((2 * row + p) * SPACING, 8)
            packed[device, parity, pair, p] = wide[parity][pl.ds(start, band), :].astype(BF16)

    def send(some):
        pltpu.make_async_copy(packed.at[some], out.at[some], sem).start()

    @pl.when(step == pl.num_programs(0) - 1)
    def _():
        for_each_tile(modes, devices, 2 * pairs, pack, send)
        pltpu.make_async_copy(packed, out, sem).wait()


def fourier(modes, field, table, devices, slots):
    band, lon_count, width = field.shape
    waves = table.shape[1]
    shape = (devices, 2, slots // 2, 2, band, width)
    return pl.pallas_call(
        fourier_kernel,
        grid_spec=pltpu.PrefetchScalarGridSpec(
            num_scalar_prefetch=1,
            grid=(band // LATS,),
            in_specs=[
                pl.BlockSpec((LATS, lon_count, width), lambda i, m: (i, 0, 0)),
                pl.BlockSpec(table.shape, lambda i, m: (0, 0, 0)),
            ],
            out_specs=pl.BlockSpec(memory_space=pl.ANY),
            scratch_shapes=[pltpu.VMEM((waves * SPACING, width), F32)] * 2
            + [pltpu.VMEM(shape, BF16), pltpu.SemaphoreType.DMA],
        ),
        out_shape=jax.ShapeDtypeStruct(shape, BF16),
        compiler_params=pltpu.CompilerParams(vmem_limit_bytes=56 * 2**20),
        cost_estimate=pl.CostEstimate(
            flops=4 * band * lon_count * waves * width,
            bytes_accessed=2 * (band * lon_count * width + 4 * waves * band * width),
            transcendentals=0,
        ),
        name="fourier",
    )(modes, field, table)


def inverse_kernel(modes, pieces, table, out, even, odd):
    step = pl.program_id(0)
    lats, lon_count, width = out.shape
    half = lon_count // 2
    waves = table.shape[2]
    devices, _, pairs, _, band, _ = pieces.shape
    wide = (even, odd)

    def unpack(device, pair, parity, row):
        for p in range(2):
            start = pl.multiple_of((2 * row + p) * SPACING, 8)
            wide[parity][pl.ds(start, band), :] = pieces[device, parity, pair, p].astype(F32)

    @pl.when(step == 0)
    def _():
        for_each_tile(modes, devices, 2 * pairs, unpack)

    sums = []
    for parity in range(2):
        columns = [
            wide[parity][pl.ds(step * lats + a, waves, stride=SPACING), :].astype(BF16)
            for a in range(lats)
        ]
        sums.append(
            jnp.dot(table[parity], jnp.concatenate(columns, axis=1), preferred_element_type=F32)
        )
    low = (sums[0] + sums[1]).astype(BF16)
    high = (sums[0] - sums[1]).astype(BF16)
    for a in range(lats):
        out[a, :half, :] = low[:, a * width : (a + 1) * width]
        out[a, half:, :] = high[:, a * width : (a + 1) * width]


def inverse(modes, pieces, table):
    band, width = pieces.shape[-2:]
    _, half, waves = table.shape
    return pl.pallas_call(
        inverse_kernel,
        grid_spec=pltpu.PrefetchScalarGridSpec(
            num_scalar_prefetch=1,
            grid=(band // LATS,),
            in_specs=[
                pl.BlockSpec(memory_space=pltpu.VMEM),
                pl.BlockSpec(table.shape, lambda i, m: (0, 0, 0)),
            ],
            out_specs=pl.BlockSpec((LATS, 2 * half, width), lambda i, m: (i, 0, 0)),
            scratch_shapes=[pltpu.VMEM((waves * SPACING, width), F32)] * 2,
        ),
        out_shape=jax.ShapeDtypeStruct((band, 2 * half, width), BF16),
        compiler_params=pltpu.CompilerParams(vmem_limit_bytes=48 * 2**20),
        name="inverse_fourier",
    )(modes, pieces, table)


def carry_kernel(mixer, gain, out):
    core = lax.axis_index("lat") & 1
    rows, width = mixer.shape[1], gain.shape[1]
    out[:rows, :] = mixer[core]
    blocks = out.shape[1] // width
    deep = gain.shape[0] // 2 // blocks
    for block in range(blocks):
        start = pl.multiple_of(core * (gain.shape[0] // 2) + block * deep, deep)
        out[rows:, block * width : (block + 1) * width] = gain[pl.ds(start, deep), :]


def carry(mixer, gain):
    rows = mixer.shape[1] + gain.size // 2 // mixer.shape[2]
    return pl.pallas_call(
        carry_kernel,
        in_specs=[pl.BlockSpec(memory_space=pltpu.VMEM)] * 2,
        out_specs=pl.BlockSpec(memory_space=pltpu.VMEM),
        out_shape=jax.ShapeDtypeStruct((rows, mixer.shape[2]), BF16),
        name="carry",
    )(mixer, gain)


def gather_kernel(mixer, gain, *rest):
    mix, gains = rest[-2:]
    width = gain.shape[1]
    chan_parts = gains.shape[0]
    channels = chan_parts * width
    core = lax.axis_index("lat") & 1
    shares = rest[: chan_parts - 1], rest[chan_parts - 1 : 2 * (chan_parts - 1)]

    def place_mixer(hops, real, imag):
        here, below = hops * width, channels + hops * width
        if real is not None:
            mix[here : here + width, :channels] = real
            mix[below : below + width, channels:] = real
        if imag is not None:
            mix[here : here + width, channels:] = imag
            mix[below : below + width, :channels] = -imag

    place_mixer(0, mixer[0], mixer[1])
    gains[0] = gain[...]
    for hops in range(1, chan_parts):
        for swap in range(2):
            share = shares[swap][hops - 1]
            deep = share.shape[0] - width
            for block in range(chan_parts):
                start = pl.multiple_of((core ^ swap) * (gain.shape[0] // 2) + block * deep, deep)
                gains[hops, pl.ds(start, deep), :] = share[
                    width:, block * width : (block + 1) * width
                ]

            @pl.when(core ^ swap == 0)
            def _():
                place_mixer(hops, share[:width, :], None)

            @pl.when(core ^ swap == 1)
            def _():
                place_mixer(hops, None, share[:width, :])


def gather(mixer, gain, shares, chan_parts):
    channels2 = 2 * mixer.shape[2]
    whole = pl.BlockSpec(memory_space=pltpu.VMEM)
    return pl.pallas_call(
        gather_kernel,
        in_specs=[whole] * (2 + len(shares)),
        out_specs=[whole] * 2,
        out_shape=[
            jax.ShapeDtypeStruct((channels2, channels2), BF16),
            jax.ShapeDtypeStruct((chan_parts,) + gain.shape, BF16),
        ],
        compiler_params=pltpu.CompilerParams(vmem_limit_bytes=16 * 2**20),
        name="gather",
    )(mixer, gain, *shares)


def spectral_kernel(
    modes, place, pieces, basis_low, basis_high, mix, gains, out, hidden, mixed, kept_low, kept_high
):
    pair = pl.program_id(0)
    pairs = pl.num_programs(0)
    lat_parts, chan_parts, _, _, _, band, width = pieces.shape
    lat_count = lat_parts * band
    channels = chan_parts * width
    degrees = basis_low.shape[1]
    block = degrees // 4
    row, chan = place[0], place[1]
    from_chan = [(chan + chan_parts - hops) % chan_parts for hops in range(chan_parts)]

    begin_mode = chan * 2 * pairs + 2 * pair
    lower = jnp.minimum(modes[begin_mode, row], modes[begin_mode + 1, row])
    higher = jnp.maximum(modes[begin_mode, row], modes[begin_mode + 1, row])

    def masked(basis, begin, count, wave):
        kept = begin + lax.broadcasted_iota(jnp.int32, (count, lat_count), 0) >= wave
        first = begin - (degrees - basis.shape[1])
        return jnp.where(kept, basis[0, first : first + count, :], jnp.zeros((), BF16))

    kept_low[...] = masked(basis_low, 0, degrees, lower)
    kept_high[:block, :] = masked(basis_high, degrees - block, block, higher)
    kept_high[block:, :] = masked(basis_high, degrees - 2 * block, block, higher)

    def analyse(wave, kept, begin, count, target, spans):
        for p in range(2):
            for first_hop in range(0, chan_parts, 2):
                columns = [
                    pieces[:, from_chan[first_hop + k], wave & 1, 0, p].reshape(lat_count, width)
                    for k in range(2)
                ]
                part = jnp.dot(
                    kept[begin : begin + count, :],
                    jnp.concatenate(columns, axis=1),
                    preferred_element_type=F32,
                )
                for k in range(2):
                    hops = first_hop + k
                    start = p * channels + hops * width
                    for offset, rows, degree in spans:
                        factor = gains[hops, degree : degree + rows, :].astype(F32)
                        hidden[target + offset : target + offset + rows, start : start + width] = (
                            part[offset : offset + rows, k * width : (k + 1) * width] * factor
                        ).astype(BF16)

    wide_low = lower < block

    @pl.when(wide_low)
    def _():
        analyse(lower, kept_low, 0, degrees, 0, [(0, degrees, 0)])
        mixed[degrees + block :, :] = jnp.zeros((block, 2 * channels), BF16)

    @pl.when(jnp.logical_not(wide_low))
    def _():
        analyse(lower, kept_low, block, degrees - block, block, [(0, degrees - block, block)])
        mixed[:block, :] = jnp.zeros((block, 2 * channels), BF16)


    @pl.when(wide_low)
    def _():
        analyse(higher, kept_high, 0, block, degrees, [(0, block, degrees - block)])

    @pl.when(jnp.logical_not(wide_low))
    def _():
        analyse(
            higher,
            kept_high,
            0,
            2 * block,
            degrees,
            [(0, block, degrees - block), (block, block, degrees - 2 * block)],
        )

    rows = pl.ds(pl.multiple_of(jnp.where(wide_low, 0, block), block), degrees + block)
    for p in range(2):
        columns = slice(p * channels, (p + 1) * channels)
        mixed[rows, columns] = jnp.dot(
            hidden[rows, :], mix[:, columns], preferred_element_type=F32
        ).astype(BF16)

    for wave, kept, begin in ((lower, kept_low, 0), (higher, kept_high, degrees)):
        for p in range(2):
            for j in range(0, chan_parts, 2):
                start = p * channels + j * width
                back = lax.dot_general(
                    kept[...],
                    mixed[begin : begin + kept.shape[0], start : start + 2 * width],
                    (((0,), (0,)), ((), ())),
                    preferred_element_type=F32,
                ).astype(BF16)
                for k in range(2):
                    out[:, j + k, wave & 1, pair, p] = back[:, k * width : (k + 1) * width].reshape(
                        lat_parts, band, width
                    )


def spectral(modes, place, pieces, basis, mix, gains):
    _, chan_parts, _, pairs, _, _, width = pieces.shape
    degrees, lat_count = basis.shape[1:]
    channels2 = 2 * chan_parts * width

    def basis_slot(which, pair, modes, place):
        begin = place[1] * 2 * pairs + 2 * pair
        swapped = (modes[begin, place[0]] > modes[begin + 1, place[0]]).astype(jnp.int32)
        return begin + (swapped if which == 0 else 1 - swapped)

    whole = pl.BlockSpec(memory_space=pltpu.VMEM)
    one_pair = pl.BlockSpec(
        pieces.shape[:3] + (1,) + pieces.shape[4:], lambda i, m, c: (0, 0, 0, i, 0, 0, 0)
    )
    return pl.pallas_call(
        spectral_kernel,
        grid_spec=pltpu.PrefetchScalarGridSpec(
            num_scalar_prefetch=2,
            grid=(pairs,),
            in_specs=[
                one_pair,
                pl.BlockSpec((1, degrees, lat_count), lambda i, m, c: (basis_slot(0, i, m, c), 0, 0)),
                pl.BlockSpec(
                    (1, degrees // 2, lat_count), lambda i, m, c: (basis_slot(1, i, m, c), 1, 0)
                ),
                whole,
                whole,
            ],
            out_specs=whole,
            scratch_shapes=[
                pltpu.VMEM((degrees + degrees // 2, channels2), BF16),
                pltpu.VMEM((degrees + degrees // 2, channels2), BF16),
                pltpu.VMEM((degrees, lat_count), BF16),
                pltpu.VMEM((degrees // 2, lat_count), BF16),
            ],
        ),
        out_shape=jax.ShapeDtypeStruct(pieces.shape, BF16),
        compiler_params=pltpu.CompilerParams(vmem_limit_bytes=40 * 2**20),
        name="spectral",
    )(modes, place, pieces, basis, basis, mix, gains)


def local(lat_parts, chan_parts, grid_field, mode_lists, lat_basis, degree_gain, channel_mixer):
    devices = lat_parts * chan_parts
    slots = lat_basis.shape[0] // chan_parts
    forward_table, back_table = folded_tables(grid_field.shape[1], mode_lists.size)
    forward_table = jnp.asarray(forward_table)
    modes = mode_lists.T
    lat_index = lax.axis_index("lat")
    place = jnp.stack([lat_index, lax.axis_index("chan")]).astype(jnp.int32)

    share = carry(channel_mixer, degree_gain)
    shares = [
        lax.ppermute(share, "chan", [(i, (i + hops) % chan_parts) for i in range(chan_parts)])
        for hops in range(1, chan_parts)
    ]
    sent = fourier(modes, grid_field, forward_table, devices, slots)
    sent, shares = lax.optimization_barrier((sent, shares))
    swapped = [lax.ppermute(s, "lat", [(i, i ^ 1) for i in range(lat_parts)]) for s in shares]
    got = lax.all_to_all(sent, ("lat", "chan"), 0, 0, tiled=True)
    got = got.reshape((lat_parts, chan_parts) + got.shape[1:])
    mix, gains = gather(channel_mixer, degree_gain, shares + swapped, chan_parts)
    back = spectral(modes, place, got, lat_basis, mix, gains)
    back = back.reshape((devices,) + back.shape[2:])
    returned = lax.all_to_all(back, ("lat", "chan"), 0, 0, tiled=True)
    return inverse(modes, returned, jnp.asarray(back_table))


def solution(mesh):
    return jax.shard_map(
        functools.partial(local, mesh.shape["lat"], mesh.shape["chan"]),
        mesh=mesh,
        in_specs=(
            P("lat", None, "chan"),
            P(),
            P("lat", None, None),
            P(None, "chan"),
            P(None, "chan", None),
        ),
        out_specs=P("lat", None, "chan"),
        check_vma=False,
    )
```

```python
import functools
import math

import jax
import jax.numpy as jnp
import ml_dtypes
import numpy as np
from jax import lax
from jax.experimental import pallas as pl
from jax.experimental.pallas import tpu as pltpu
from jax.sharding import PartitionSpec as P

BF16 = jnp.bfloat16
F32 = jnp.float32
FOURIER_LATS = 8
LATS = 4
SPACING = 24


def folded_tables(lon_count, wave_count):
    half = lon_count // 2
    waves = np.arange(wave_count).reshape(-1, 2).T
    phases = (waves[:, :, None] * np.arange(half)[None, None, :]) % lon_count
    angles = phases * (2.0 * math.pi / lon_count)
    factor = 1.0 / math.sqrt(lon_count)
    table = np.stack([np.cos(angles) * factor, -np.sin(angles) * factor], axis=2)
    table = table.reshape(2, wave_count, half).astype(np.float32).astype(ml_dtypes.bfloat16)
    return table, np.ascontiguousarray(table.transpose(0, 2, 1))


def for_each_tile(modes, devices, slots, move, after=None):
    per_row = modes.shape[0] // slots
    last = modes.shape[0] * modes.shape[1] - 1

    def row_step(row, carry):
        for pair in range(modes.shape[0] // 2):
            mode = modes[2 * pair, row]
            even_row = jnp.where(mode & 1 == 1, last - mode, mode) >> 1
            device = row * per_row + 2 * pair // slots
            place = 2 * pair % slots // 2
            move(device, place, 0, even_row)
            move(device, place, 1, (last >> 1) - even_row)
        if after is not None:
            after(pl.ds(pl.multiple_of(row * per_row, per_row), per_row))
        return carry

    lax.fori_loop(0, devices // per_row, row_step, 0)


def fourier_kernel(modes, field, table, out, even, odd, packed, sem):
    step = pl.program_id(0)
    lats, lon_count, width = field.shape
    half = lon_count // 2
    waves = table.shape[1]
    devices, _, pairs, _, band, _ = out.shape
    wide = (even, odd)
    low = jnp.concatenate([field[a, :half, :] for a in range(lats)], axis=1)
    high = jnp.concatenate([field[a, half:, :] for a in range(lats)], axis=1)
    for parity in range(2):
        folded = low + high if parity == 0 else low - high
        result = jnp.dot(table[parity], folded, preferred_element_type=F32)
        for a in range(lats):
            rows = pl.ds(step * lats + a, waves, stride=SPACING)
            wide[parity][rows, :] = result[:, a * width : (a + 1) * width]

    def pack(device, pair, parity, row):
        for p in range(2):
            start = pl.multiple_of((2 * row + p) * SPACING, 8)
            packed[device, parity, pair, p] = wide[parity][pl.ds(start, band), :].astype(BF16)

    def send(some):
        pltpu.make_async_copy(packed.at[some], out.at[some], sem).start()

    @pl.when(step == pl.num_programs(0) - 1)
    def _():
        for_each_tile(modes, devices, 2 * pairs, pack, send)
        pltpu.make_async_copy(packed, out, sem).wait()


def fourier(modes, field, table, devices, slots):
    band, lon_count, width = field.shape
    waves = table.shape[1]
    shape = (devices, 2, slots // 2, 2, band, width)
    return pl.pallas_call(
        fourier_kernel,
        grid=(band // FOURIER_LATS,),
        in_specs=[
            pl.BlockSpec(memory_space=pltpu.SMEM),
            pl.BlockSpec((FOURIER_LATS, lon_count, width), lambda i: (i, 0, 0)),
            pl.BlockSpec(table.shape, lambda i: (0, 0, 0)),
        ],
        out_specs=pl.BlockSpec(memory_space=pl.ANY),
        scratch_shapes=[pltpu.VMEM((waves * SPACING, width), F32)] * 2
        + [pltpu.VMEM(shape, BF16), pltpu.SemaphoreType.DMA],
        out_shape=jax.ShapeDtypeStruct(shape, BF16),
        compiler_params=pltpu.CompilerParams(vmem_limit_bytes=56 * 2**20),
        cost_estimate=pl.CostEstimate(
            flops=4 * band * lon_count * waves * width,
            bytes_accessed=2 * (band * lon_count * width + 4 * waves * band * width),
            transcendentals=0,
        ),
        name="fourier",
    )(modes, field, table)


def inverse_kernel(modes, pieces, table, out, even, odd):
    step = pl.program_id(0)
    lats, lon_count, width = out.shape
    half = lon_count // 2
    waves = table.shape[2]
    devices, _, pairs, _, band, _ = pieces.shape
    wide = (even, odd)

    def unpack(device, pair, parity, row):
        for p in range(2):
            start = pl.multiple_of((2 * row + p) * SPACING, 8)
            wide[parity][pl.ds(start, band), :] = pieces[device, parity, pair, p].astype(F32)

    @pl.when(step == 0)
    def _():
        for_each_tile(modes, devices, 2 * pairs, unpack)

    sums = []
    for parity in range(2):
        columns = [
            wide[parity][pl.ds(step * lats + a, waves, stride=SPACING), :].astype(BF16)
            for a in range(lats)
        ]
        sums.append(
            jnp.dot(table[parity], jnp.concatenate(columns, axis=1), preferred_element_type=F32)
        )
    low = (sums[0] + sums[1]).astype(BF16)
    high = (sums[0] - sums[1]).astype(BF16)
    for a in range(lats):
        out[a, :half, :] = low[:, a * width : (a + 1) * width]
        out[a, half:, :] = high[:, a * width : (a + 1) * width]


def inverse(modes, pieces, table):
    band, width = pieces.shape[-2:]
    _, half, waves = table.shape
    return pl.pallas_call(
        inverse_kernel,
        grid_spec=pltpu.PrefetchScalarGridSpec(
            num_scalar_prefetch=1,
            grid=(band // LATS,),
            in_specs=[
                pl.BlockSpec(memory_space=pltpu.VMEM),
                pl.BlockSpec(table.shape, lambda i, m: (0, 0, 0)),
            ],
            out_specs=pl.BlockSpec((LATS, 2 * half, width), lambda i, m: (i, 0, 0)),
            scratch_shapes=[pltpu.VMEM((waves * SPACING, width), F32)] * 2,
        ),
        out_shape=jax.ShapeDtypeStruct((band, 2 * half, width), BF16),
        compiler_params=pltpu.CompilerParams(vmem_limit_bytes=48 * 2**20),
        name="inverse_fourier",
    )(modes, pieces, table)


def carry_kernel(mixer, gain, out):
    core = lax.axis_index("lat") & 1
    rows, width = mixer.shape[1], gain.shape[1]
    out[:rows, :] = mixer[core]
    blocks = out.shape[1] // width
    deep = gain.shape[0] // 2 // blocks
    for block in range(blocks):
        start = pl.multiple_of(core * (gain.shape[0] // 2) + block * deep, deep)
        out[rows:, block * width : (block + 1) * width] = gain[pl.ds(start, deep), :]


def carry(mixer, gain):
    rows = mixer.shape[1] + gain.size // 2 // mixer.shape[2]
    return pl.pallas_call(
        carry_kernel,
        in_specs=[pl.BlockSpec(memory_space=pltpu.VMEM)] * 2,
        out_specs=pl.BlockSpec(memory_space=pltpu.VMEM),
        out_shape=jax.ShapeDtypeStruct((rows, mixer.shape[2]), BF16),
        name="carry",
    )(mixer, gain)


def gather_kernel(mixer, gain, *rest):
    mix, gains = rest[-2:]
    width = gain.shape[1]
    chan_parts = gains.shape[0]
    channels = chan_parts * width
    core = lax.axis_index("lat") & 1
    shares = rest[: chan_parts - 1], rest[chan_parts - 1 : 2 * (chan_parts - 1)]

    def place_mixer(hops, real, imag):
        here, below = hops * width, channels + hops * width
        if real is not None:
            mix[here : here + width, :channels] = real
            mix[below : below + width, channels:] = real
        if imag is not None:
            mix[here : here + width, channels:] = imag
            mix[below : below + width, :channels] = -imag

    place_mixer(0, mixer[0], mixer[1])
    gains[0] = gain[...]
    for hops in range(1, chan_parts):
        for swap in range(2):
            share = shares[swap][hops - 1]
            deep = share.shape[0] - width
            for block in range(chan_parts):
                start = pl.multiple_of((core ^ swap) * (gain.shape[0] // 2) + block * deep, deep)
                gains[hops, pl.ds(start, deep), :] = share[
                    width:, block * width : (block + 1) * width
                ]

            @pl.when(core ^ swap == 0)
            def _():
                place_mixer(hops, share[:width, :], None)

            @pl.when(core ^ swap == 1)
            def _():
                place_mixer(hops, None, share[:width, :])


def gather(mixer, gain, shares, chan_parts):
    channels2 = 2 * mixer.shape[2]
    whole = pl.BlockSpec(memory_space=pltpu.VMEM)
    return pl.pallas_call(
        gather_kernel,
        in_specs=[whole] * (2 + len(shares)),
        out_specs=[whole] * 2,
        out_shape=[
            jax.ShapeDtypeStruct((channels2, channels2), BF16),
            jax.ShapeDtypeStruct((chan_parts,) + gain.shape, BF16),
        ],
        compiler_params=pltpu.CompilerParams(vmem_limit_bytes=16 * 2**20),
        name="gather",
    )(mixer, gain, *shares)


def spectral_kernel(
    modes, place, pieces, basis_low, basis_high, mix, gains, out, hidden, mixed, kept_low, kept_high
):
    pair = pl.program_id(0)
    pairs = pl.num_programs(0)
    lat_parts, chan_parts, _, _, _, band, width = pieces.shape
    lat_count = lat_parts * band
    channels = chan_parts * width
    degrees = basis_low.shape[1]
    block = degrees // 4
    row, chan = place[0], place[1]
    from_chan = [(chan + chan_parts - hops) % chan_parts for hops in range(chan_parts)]

    begin_mode = chan * 2 * pairs + 2 * pair
    lower = jnp.minimum(modes[begin_mode, row], modes[begin_mode + 1, row])
    higher = jnp.maximum(modes[begin_mode, row], modes[begin_mode + 1, row])

    def masked(basis, begin, count, wave):
        kept = begin + lax.broadcasted_iota(jnp.int32, (count, lat_count), 0) >= wave
        first = begin - (degrees - basis.shape[1])
        return jnp.where(kept, basis[0, first : first + count, :], jnp.zeros((), BF16))

    kept_low[...] = masked(basis_low, 0, degrees, lower)
    kept_high[:block, :] = masked(basis_high, degrees - block, block, higher)
    kept_high[block:, :] = masked(basis_high, degrees - 2 * block, block, higher)

    def analyse(wave, kept, begin, count, target, spans):
        for p in range(2):
            for first_hop in range(0, chan_parts, 2):
                columns = [
                    pieces[:, from_chan[first_hop + k], wave & 1, 0, p].reshape(lat_count, width)
                    for k in range(2)
                ]
                part = jnp.dot(
                    kept[begin : begin + count, :],
                    jnp.concatenate(columns, axis=1),
                    preferred_element_type=F32,
                )
                for k in range(2):
                    hops = first_hop + k
                    start = p * channels + hops * width
                    for offset, rows, degree in spans:
                        factor = gains[hops, degree : degree + rows, :].astype(F32)
                        hidden[target + offset : target + offset + rows, start : start + width] = (
                            part[offset : offset + rows, k * width : (k + 1) * width] * factor
                        ).astype(BF16)

    wide_low = lower < block

    @pl.when(wide_low)
    def _():
        analyse(lower, kept_low, 0, degrees, 0, [(0, degrees, 0)])
        mixed[degrees + block :, :] = jnp.zeros((block, 2 * channels), BF16)

    @pl.when(jnp.logical_not(wide_low))
    def _():
        analyse(lower, kept_low, block, degrees - block, block, [(0, degrees - block, block)])
        mixed[:block, :] = jnp.zeros((block, 2 * channels), BF16)


    @pl.when(wide_low)
    def _():
        analyse(higher, kept_high, 0, block, degrees, [(0, block, degrees - block)])

    @pl.when(jnp.logical_not(wide_low))
    def _():
        analyse(
            higher,
            kept_high,
            0,
            2 * block,
            degrees,
            [(0, block, degrees - block), (block, block, degrees - 2 * block)],
        )

    rows = pl.ds(pl.multiple_of(jnp.where(wide_low, 0, block), block), degrees + block)
    for p in range(2):
        columns = slice(p * channels, (p + 1) * channels)
        mixed[rows, columns] = jnp.dot(
            hidden[rows, :], mix[:, columns], preferred_element_type=F32
        ).astype(BF16)

    for wave, kept, begin in ((lower, kept_low, 0), (higher, kept_high, degrees)):
        for p in range(2):
            for j in range(0, chan_parts, 2):
                start = p * channels + j * width
                back = lax.dot_general(
                    kept[...],
                    mixed[begin : begin + kept.shape[0], start : start + 2 * width],
                    (((0,), (0,)), ((), ())),
                    preferred_element_type=F32,
                ).astype(BF16)
                for k in range(2):
                    out[:, j + k, wave & 1, pair, p] = back[:, k * width : (k + 1) * width].reshape(
                        lat_parts, band, width
                    )


def spectral(modes, place, pieces, basis, mix, gains):
    _, chan_parts, _, pairs, _, _, width = pieces.shape
    degrees, lat_count = basis.shape[1:]
    channels2 = 2 * chan_parts * width

    def basis_slot(which, pair, modes, place):
        begin = place[1] * 2 * pairs + 2 * pair
        swapped = (modes[begin, place[0]] > modes[begin + 1, place[0]]).astype(jnp.int32)
        return begin + (swapped if which == 0 else 1 - swapped)

    whole = pl.BlockSpec(memory_space=pltpu.VMEM)
    one_pair = pl.BlockSpec(
        pieces.shape[:3] + (1,) + pieces.shape[4:], lambda i, m, c: (0, 0, 0, i, 0, 0, 0)
    )
    return pl.pallas_call(
        spectral_kernel,
        grid_spec=pltpu.PrefetchScalarGridSpec(
            num_scalar_prefetch=2,
            grid=(pairs,),
            in_specs=[
                one_pair,
                pl.BlockSpec((1, degrees, lat_count), lambda i, m, c: (basis_slot(0, i, m, c), 0, 0)),
                pl.BlockSpec(
                    (1, degrees // 2, lat_count), lambda i, m, c: (basis_slot(1, i, m, c), 1, 0)
                ),
                whole,
                whole,
            ],
            out_specs=whole,
            scratch_shapes=[
                pltpu.VMEM((degrees + degrees // 2, channels2), BF16),
                pltpu.VMEM((degrees + degrees // 2, channels2), BF16),
                pltpu.VMEM((degrees, lat_count), BF16),
                pltpu.VMEM((degrees // 2, lat_count), BF16),
            ],
        ),
        out_shape=jax.ShapeDtypeStruct(pieces.shape, BF16),
        compiler_params=pltpu.CompilerParams(vmem_limit_bytes=40 * 2**20),
        name="spectral",
    )(modes, place, pieces, basis, basis, mix, gains)


def local(lat_parts, chan_parts, grid_field, mode_lists, lat_basis, degree_gain, channel_mixer):
    devices = lat_parts * chan_parts
    slots = lat_basis.shape[0] // chan_parts
    forward_table, back_table = folded_tables(grid_field.shape[1], mode_lists.size)
    forward_table = jnp.asarray(forward_table)
    modes = mode_lists.T
    lat_index = lax.axis_index("lat")
    place = jnp.stack([lat_index, lax.axis_index("chan")]).astype(jnp.int32)

    share = carry(channel_mixer, degree_gain)
    shares = [
        lax.ppermute(share, "chan", [(i, (i + hops) % chan_parts) for i in range(chan_parts)])
        for hops in range(1, chan_parts)
    ]
    sent = fourier(modes, grid_field, forward_table, devices, slots)
    sent, shares = lax.optimization_barrier((sent, shares))
    swapped = [lax.ppermute(s, "lat", [(i, i ^ 1) for i in range(lat_parts)]) for s in shares]
    got = lax.all_to_all(sent, ("lat", "chan"), 0, 0, tiled=True)
    got = got.reshape((lat_parts, chan_parts) + got.shape[1:])
    mix, gains = gather(channel_mixer, degree_gain, shares + swapped, chan_parts)
    back = spectral(modes, place, got, lat_basis, mix, gains)
    back = back.reshape((devices,) + back.shape[2:])
    returned = lax.all_to_all(back, ("lat", "chan"), 0, 0, tiled=True)
    return inverse(modes, returned, jnp.asarray(back_table))


def solution(mesh):
    return jax.shard_map(
        functools.partial(local, mesh.shape["lat"], mesh.shape["chan"]),
        mesh=mesh,
        in_specs=(
            P("lat", None, "chan"),
            P(),
            P("lat", None, None),
            P(None, "chan"),
            P(None, "chan", None),
        ),
        out_specs=P("lat", None, "chan"),
        check_vma=False,
    )
```

```python
import functools
import math

import jax
import jax.numpy as jnp
import ml_dtypes
import numpy as np
from jax import lax
from jax.experimental import pallas as pl
from jax.experimental.pallas import tpu as pltpu
from jax.sharding import PartitionSpec as P

BF16 = jnp.bfloat16
F32 = jnp.float32
FOURIER_LATS = 8
LATS = 4
SPACING = 24


def folded_tables(lon_count, wave_count):
    half = lon_count // 2
    waves = np.arange(wave_count).reshape(-1, 2).T
    phases = (waves[:, :, None] * np.arange(half)[None, None, :]) % lon_count
    angles = phases * (2.0 * math.pi / lon_count)
    factor = 1.0 / math.sqrt(lon_count)
    table = np.stack([np.cos(angles) * factor, -np.sin(angles) * factor], axis=2)
    table = table.reshape(2, wave_count, half).astype(np.float32).astype(ml_dtypes.bfloat16)
    return table, np.ascontiguousarray(table.transpose(0, 2, 1))


def for_each_tile(modes, devices, slots, move, after=None):
    per_row = modes.shape[0] // slots
    last = modes.shape[0] * modes.shape[1] - 1

    def row_step(row, carry):
        for pair in range(modes.shape[0] // 2):
            mode = modes[2 * pair, row]
            even_row = jnp.where(mode & 1 == 1, last - mode, mode) >> 1
            device = row * per_row + 2 * pair // slots
            place = 2 * pair % slots // 2
            move(device, place, 0, even_row)
            move(device, place, 1, (last >> 1) - even_row)
        if after is not None:
            after(pl.ds(pl.multiple_of(row * per_row, per_row), per_row))
        return carry

    lax.fori_loop(0, devices // per_row, row_step, 0)


def fourier_kernel(modes, field, table, out, even, odd, packed, sem):
    step = pl.program_id(0)
    lats, lon_count, width = field.shape
    half = lon_count // 2
    waves = table.shape[1]
    devices, _, pairs, _, band, _ = out.shape
    wide = (even, odd)
    low = jnp.concatenate([field[a, :half, :] for a in range(lats)], axis=1)
    high = jnp.concatenate([field[a, half:, :] for a in range(lats)], axis=1)
    for parity in range(2):
        folded = low + high if parity == 0 else low - high
        result = jnp.dot(table[parity], folded, preferred_element_type=F32)
        for a in range(lats):
            rows = pl.ds(step * lats + a, waves, stride=SPACING)
            wide[parity][rows, :] = result[:, a * width : (a + 1) * width]

    def pack(device, pair, parity, row):
        for p in range(2):
            start = pl.multiple_of((2 * row + p) * SPACING, 8)
            packed[device, parity, pair, p] = wide[parity][pl.ds(start, band), :].astype(BF16)

    def send(some):
        pltpu.make_async_copy(packed.at[some], out.at[some], sem).start()

    @pl.when(step == pl.num_programs(0) - 1)
    def _():
        for_each_tile(modes, devices, 2 * pairs, pack, send)
        pltpu.make_async_copy(packed, out, sem).wait()


def fourier(modes, field, table, devices, slots):
    band, lon_count, width = field.shape
    waves = table.shape[1]
    shape = (devices, 2, slots // 2, 2, band, width)
    return pl.pallas_call(
        fourier_kernel,
        grid=(band // FOURIER_LATS,),
        in_specs=[
            pl.BlockSpec(memory_space=pltpu.SMEM),
            pl.BlockSpec((FOURIER_LATS, lon_count, width), lambda i: (i, 0, 0)),
            pl.BlockSpec(table.shape, lambda i: (0, 0, 0)),
        ],
        out_specs=pl.BlockSpec(memory_space=pl.ANY),
        scratch_shapes=[pltpu.VMEM((waves * SPACING, width), F32)] * 2
        + [pltpu.VMEM(shape, BF16), pltpu.SemaphoreType.DMA],
        out_shape=jax.ShapeDtypeStruct(shape, BF16),
        compiler_params=pltpu.CompilerParams(vmem_limit_bytes=56 * 2**20),
        cost_estimate=pl.CostEstimate(
            flops=4 * band * lon_count * waves * width,
            bytes_accessed=2 * (band * lon_count * width + 4 * waves * band * width),
            transcendentals=0,
        ),
        name="fourier",
    )(modes, field, table)


def inverse_kernel(modes, pieces, table, out, even, odd):
    step = pl.program_id(0)
    lats, lon_count, width = out.shape
    half = lon_count // 2
    waves = table.shape[2]
    devices, _, pairs, _, band, _ = pieces.shape
    wide = (even, odd)

    def unpack(device, pair, parity, row):
        for p in range(2):
            start = pl.multiple_of((2 * row + p) * SPACING, 8)
            wide[parity][pl.ds(start, band), :] = pieces[device, parity, pair, p].astype(F32)

    @pl.when(step == 0)
    def _():
        for_each_tile(modes, devices, 2 * pairs, unpack)

    sums = []
    for parity in range(2):
        columns = [
            wide[parity][pl.ds(step * lats + a, waves, stride=SPACING), :].astype(BF16)
            for a in range(lats)
        ]
        sums.append(
            jnp.dot(table[parity], jnp.concatenate(columns, axis=1), preferred_element_type=F32)
        )
    low = (sums[0] + sums[1]).astype(BF16)
    high = (sums[0] - sums[1]).astype(BF16)
    for a in range(lats):
        out[a, :half, :] = low[:, a * width : (a + 1) * width]
        out[a, half:, :] = high[:, a * width : (a + 1) * width]


def inverse(modes, pieces, table):
    band, width = pieces.shape[-2:]
    _, half, waves = table.shape
    return pl.pallas_call(
        inverse_kernel,
        grid_spec=pltpu.PrefetchScalarGridSpec(
            num_scalar_prefetch=1,
            grid=(band // LATS,),
            in_specs=[
                pl.BlockSpec(memory_space=pltpu.VMEM),
                pl.BlockSpec(table.shape, lambda i, m: (0, 0, 0)),
            ],
            out_specs=pl.BlockSpec((LATS, 2 * half, width), lambda i, m: (i, 0, 0)),
            scratch_shapes=[pltpu.VMEM((waves * SPACING, width), F32)] * 2,
        ),
        out_shape=jax.ShapeDtypeStruct((band, 2 * half, width), BF16),
        compiler_params=pltpu.CompilerParams(vmem_limit_bytes=48 * 2**20),
        name="inverse_fourier",
    )(modes, pieces, table)


def carry_kernel(mixer, gain, out):
    core = lax.axis_index("lat") & 1
    rows, width = mixer.shape[1], gain.shape[1]
    out[:rows, :] = mixer[core]
    blocks = out.shape[1] // width
    deep = gain.shape[0] // 2 // blocks
    for block in range(blocks):
        start = pl.multiple_of(core * (gain.shape[0] // 2) + block * deep, deep)
        out[rows:, block * width : (block + 1) * width] = gain[pl.ds(start, deep), :]


def carry(mixer, gain):
    rows = mixer.shape[1] + gain.size // 2 // mixer.shape[2]
    return pl.pallas_call(
        carry_kernel,
        in_specs=[pl.BlockSpec(memory_space=pltpu.VMEM)] * 2,
        out_specs=pl.BlockSpec(memory_space=pltpu.VMEM),
        out_shape=jax.ShapeDtypeStruct((rows, mixer.shape[2]), BF16),
        name="carry",
    )(mixer, gain)


def gather_kernel(mixer, gain, *rest):
    mix, gains = rest[-2:]
    width = gain.shape[1]
    chan_parts = gains.shape[0]
    channels = chan_parts * width
    core = lax.axis_index("lat") & 1
    shares = rest[: chan_parts - 1], rest[chan_parts - 1 : 2 * (chan_parts - 1)]

    def place_mixer(hops, real, imag):
        here, below = hops * width, channels + hops * width
        if real is not None:
            mix[here : here + width, :channels] = real
            mix[below : below + width, channels:] = real
        if imag is not None:
            mix[here : here + width, channels:] = imag
            mix[below : below + width, :channels] = -imag

    place_mixer(0, mixer[0], mixer[1])
    gains[0] = gain[...]
    for hops in range(1, chan_parts):
        for swap in range(2):
            share = shares[swap][hops - 1]
            deep = share.shape[0] - width
            for block in range(chan_parts):
                start = pl.multiple_of((core ^ swap) * (gain.shape[0] // 2) + block * deep, deep)
                gains[hops, pl.ds(start, deep), :] = share[
                    width:, block * width : (block + 1) * width
                ]

            @pl.when(core ^ swap == 0)
            def _():
                place_mixer(hops, share[:width, :], None)

            @pl.when(core ^ swap == 1)
            def _():
                place_mixer(hops, None, share[:width, :])


def gather(mixer, gain, shares, chan_parts):
    channels2 = 2 * mixer.shape[2]
    whole = pl.BlockSpec(memory_space=pltpu.VMEM)
    return pl.pallas_call(
        gather_kernel,
        in_specs=[whole] * (2 + len(shares)),
        out_specs=[whole] * 2,
        out_shape=[
            jax.ShapeDtypeStruct((channels2, channels2), BF16),
            jax.ShapeDtypeStruct((chan_parts,) + gain.shape, BF16),
        ],
        compiler_params=pltpu.CompilerParams(vmem_limit_bytes=16 * 2**20),
        name="gather",
    )(mixer, gain, *shares)


def prepare_kernel(modes, place, basis_low, basis_high, kept):
    row, chan = place[0], place[1]
    pairs = pl.num_programs(0)
    degrees, lat_count = basis_low.shape[1:]
    block = degrees // 4
    begin_mode = chan * 2 * pairs + 2 * pl.program_id(0)
    lower = jnp.minimum(modes[begin_mode, row], modes[begin_mode + 1, row])
    higher = jnp.maximum(modes[begin_mode, row], modes[begin_mode + 1, row])

    def masked(basis, begin, count, wave):
        keep = begin + lax.broadcasted_iota(jnp.int32, (count, lat_count), 0) >= wave
        first = begin - (degrees - basis.shape[1])
        return jnp.where(keep, basis[0, first : first + count, :], jnp.zeros((), BF16))

    kept[0, :degrees, :] = masked(basis_low, 0, degrees, lower)
    kept[0, degrees : degrees + block, :] = masked(basis_high, degrees - block, block, higher)
    kept[0, degrees + block :, :] = masked(basis_high, degrees - 2 * block, block, higher)


def prepare(modes, place, basis, pairs):
    degrees, lat_count = basis.shape[1:]

    def basis_slot(which, pair, modes, place):
        begin = place[1] * 2 * pairs + 2 * pair
        swapped = (modes[begin, place[0]] > modes[begin + 1, place[0]]).astype(jnp.int32)
        return begin + (swapped if which == 0 else 1 - swapped)

    low, high = (1, degrees, lat_count), (1, degrees // 2, lat_count)
    return pl.pallas_call(
        prepare_kernel,
        grid_spec=pltpu.PrefetchScalarGridSpec(
            num_scalar_prefetch=2,
            grid=(pairs,),
            in_specs=[
                pl.BlockSpec(low, lambda i, m, c: (basis_slot(0, i, m, c), 0, 0)),
                pl.BlockSpec(high, lambda i, m, c: (basis_slot(1, i, m, c), 1, 0)),
            ],
            out_specs=pl.BlockSpec(
                (1, degrees + degrees // 2, lat_count), lambda i, m, c: (i, 0, 0)
            ),
        ),
        out_shape=jax.ShapeDtypeStruct((pairs, degrees + degrees // 2, lat_count), BF16),
        compiler_params=pltpu.CompilerParams(vmem_limit_bytes=54 * 2**20),
        name="prepare",
    )(modes, place, basis, basis)


def spectral_kernel(
    modes, place, pieces, kept_block, mix, gains, out, hidden, mixed
):
    pair = pl.program_id(0)
    pairs = pl.num_programs(0)
    lat_parts, chan_parts, _, _, _, band, width = pieces.shape
    lat_count = lat_parts * band
    channels = chan_parts * width
    degrees = gains.shape[1]
    kept_low = kept_block.at[0, pl.ds(0, degrees)]
    kept_high = kept_block.at[0, pl.ds(degrees, degrees // 2)]
    block = degrees // 4
    row, chan = place[0], place[1]
    from_chan = [(chan + chan_parts - hops) % chan_parts for hops in range(chan_parts)]

    begin_mode = chan * 2 * pairs + 2 * pair
    lower = jnp.minimum(modes[begin_mode, row], modes[begin_mode + 1, row])
    higher = jnp.maximum(modes[begin_mode, row], modes[begin_mode + 1, row])

    def analyse(wave, kept, begin, count, target, spans):
        for p in range(2):
            for first_hop in range(0, chan_parts, 2):
                columns = [
                    pieces[:, from_chan[first_hop + k], wave & 1, 0, p].reshape(lat_count, width)
                    for k in range(2)
                ]
                part = jnp.dot(
                    kept[begin : begin + count, :],
                    jnp.concatenate(columns, axis=1),
                    preferred_element_type=F32,
                )
                for k in range(2):
                    hops = first_hop + k
                    start = p * channels + hops * width
                    for offset, rows, degree in spans:
                        factor = gains[hops, degree : degree + rows, :].astype(F32)
                        hidden[target + offset : target + offset + rows, start : start + width] = (
                            part[offset : offset + rows, k * width : (k + 1) * width] * factor
                        ).astype(BF16)

    wide_low = lower < block

    @pl.when(wide_low)
    def _():
        analyse(lower, kept_low, 0, degrees, 0, [(0, degrees, 0)])
        mixed[degrees + block :, :] = jnp.zeros((block, 2 * channels), BF16)

    @pl.when(jnp.logical_not(wide_low))
    def _():
        analyse(lower, kept_low, block, degrees - block, block, [(0, degrees - block, block)])
        mixed[:block, :] = jnp.zeros((block, 2 * channels), BF16)


    @pl.when(wide_low)
    def _():
        analyse(higher, kept_high, 0, block, degrees, [(0, block, degrees - block)])

    @pl.when(jnp.logical_not(wide_low))
    def _():
        analyse(
            higher,
            kept_high,
            0,
            2 * block,
            degrees,
            [(0, block, degrees - block), (block, block, degrees - 2 * block)],
        )

    rows = pl.ds(pl.multiple_of(jnp.where(wide_low, 0, block), block), degrees + block)
    for p in range(2):
        columns = slice(p * channels, (p + 1) * channels)
        mixed[rows, columns] = jnp.dot(
            hidden[rows, :], mix[:, columns], preferred_element_type=F32
        ).astype(BF16)

    for wave, kept, begin in ((lower, kept_low, 0), (higher, kept_high, degrees)):
        for p in range(2):
            for j in range(0, chan_parts, 2):
                start = p * channels + j * width
                back = lax.dot_general(
                    kept[...],
                    mixed[begin : begin + kept.shape[0], start : start + 2 * width],
                    (((0,), (0,)), ((), ())),
                    preferred_element_type=F32,
                ).astype(BF16)
                for k in range(2):
                    out[:, j + k, wave & 1, pair, p] = back[:, k * width : (k + 1) * width].reshape(
                        lat_parts, band, width
                    )


def spectral(modes, place, pieces, kept, mix, gains):
    pairs, rows, lat_count = kept.shape
    whole = pl.BlockSpec(memory_space=pltpu.VMEM)
    scalars = pl.BlockSpec(memory_space=pltpu.SMEM)
    one_pair = pl.BlockSpec(
        pieces.shape[:3] + (1,) + pieces.shape[4:], lambda i: (0, 0, 0, i, 0, 0, 0)
    )
    return pl.pallas_call(
        spectral_kernel,
        grid=(pairs,),
        in_specs=[
            scalars,
            scalars,
            one_pair,
            pl.BlockSpec((1, rows, lat_count), lambda i: (i, 0, 0)),
            whole,
            whole,
        ],
        out_specs=whole,
        scratch_shapes=[
            pltpu.VMEM((rows, mix.shape[0]), BF16),
            pltpu.VMEM((rows, mix.shape[0]), BF16),
        ],
        out_shape=jax.ShapeDtypeStruct(pieces.shape, BF16),
        compiler_params=pltpu.CompilerParams(vmem_limit_bytes=40 * 2**20),
        name="spectral",
    )(modes, place, pieces, kept, mix, gains)


def local(lat_parts, chan_parts, grid_field, mode_lists, lat_basis, degree_gain, channel_mixer):
    devices = lat_parts * chan_parts
    slots = lat_basis.shape[0] // chan_parts
    forward_table, back_table = folded_tables(grid_field.shape[1], mode_lists.size)
    forward_table = jnp.asarray(forward_table)
    modes = mode_lists.T
    lat_index = lax.axis_index("lat")
    place = jnp.stack([lat_index, lax.axis_index("chan")]).astype(jnp.int32)

    share = carry(channel_mixer, degree_gain)
    shares = [
        lax.ppermute(share, "chan", [(i, (i + hops) % chan_parts) for i in range(chan_parts)])
        for hops in range(1, chan_parts)
    ]
    sent = fourier(modes, grid_field, forward_table, devices, slots)
    sent, shares = lax.optimization_barrier((sent, shares))
    swapped = [lax.ppermute(s, "lat", [(i, i ^ 1) for i in range(lat_parts)]) for s in shares]
    got = lax.all_to_all(sent, ("lat", "chan"), 0, 0, tiled=True)
    got = got.reshape((lat_parts, chan_parts) + got.shape[1:])
    mix, gains = gather(channel_mixer, degree_gain, shares + swapped, chan_parts)
    late_modes, late_place, _ = lax.optimization_barrier((modes, place, swapped))
    kept = prepare(late_modes, late_place, lat_basis, slots // 2)
    back = spectral(late_modes, late_place, got, kept, mix, gains)
    back = back.reshape((devices,) + back.shape[2:])
    returned = lax.all_to_all(back, ("lat", "chan"), 0, 0, tiled=True)
    return inverse(modes, returned, jnp.asarray(back_table))


def solution(mesh):
    return jax.shard_map(
        functools.partial(local, mesh.shape["lat"], mesh.shape["chan"]),
        mesh=mesh,
        in_specs=(
            P("lat", None, "chan"),
            P(),
            P("lat", None, None),
            P(None, "chan"),
            P(None, "chan", None),
        ),
        out_specs=P("lat", None, "chan"),
        check_vma=False,
    )
```

```python
import functools
import math

import jax
import jax.numpy as jnp
import ml_dtypes
import numpy as np
from jax import lax
from jax.experimental import pallas as pl
from jax.experimental.pallas import tpu as pltpu
from jax.sharding import PartitionSpec as P

BF16 = jnp.bfloat16
F32 = jnp.float32
FOURIER_LATS = 8
LATS = 4
SPACING = 24


def folded_tables(lon_count, wave_count):
    half = lon_count // 2
    waves = np.arange(wave_count).reshape(-1, 2).T
    phases = (waves[:, :, None] * np.arange(half)[None, None, :]) % lon_count
    angles = phases * (2.0 * math.pi / lon_count)
    factor = 1.0 / math.sqrt(lon_count)
    table = np.stack([np.cos(angles) * factor, -np.sin(angles) * factor], axis=2)
    table = table.reshape(2, wave_count, half).astype(np.float32).astype(ml_dtypes.bfloat16)
    return table, np.ascontiguousarray(table.transpose(0, 2, 1))


def for_each_tile(modes, devices, slots, move, after=None):
    per_row = modes.shape[0] // slots
    last = modes.shape[0] * modes.shape[1] - 1

    def row_step(row, carry):
        for pair in range(modes.shape[0] // 2):
            mode = modes[2 * pair, row]
            even_row = jnp.where(mode & 1 == 1, last - mode, mode) >> 1
            device = row * per_row + 2 * pair // slots
            place = 2 * pair % slots // 2
            move(device, place, 0, even_row)
            move(device, place, 1, (last >> 1) - even_row)
        if after is not None:
            after(pl.ds(pl.multiple_of(row * per_row, per_row), per_row))
        return carry

    lax.fori_loop(0, devices // per_row, row_step, 0)


def fourier_kernel(modes, field, table, out, even, odd, packed, sem):
    step = pl.program_id(0)
    lats, lon_count, width = field.shape
    half = lon_count // 2
    waves = table.shape[1]
    devices, _, pairs, _, band, _ = out.shape
    wide = (even, odd)
    low = jnp.concatenate([field[a, :half, :] for a in range(lats)], axis=1)
    high = jnp.concatenate([field[a, half:, :] for a in range(lats)], axis=1)
    for parity in range(2):
        folded = low + high if parity == 0 else low - high
        result = jnp.dot(table[parity], folded, preferred_element_type=F32)
        for a in range(lats):
            rows = pl.ds(step * lats + a, waves, stride=SPACING)
            wide[parity][rows, :] = result[:, a * width : (a + 1) * width]

    def pack(device, pair, parity, row):
        for p in range(2):
            start = pl.multiple_of((2 * row + p) * SPACING, 8)
            packed[device, parity, pair, p] = wide[parity][pl.ds(start, band), :].astype(BF16)

    def send(some):
        pltpu.make_async_copy(packed.at[some], out.at[some], sem).start()

    @pl.when(step == pl.num_programs(0) - 1)
    def _():
        for_each_tile(modes, devices, 2 * pairs, pack, send)
        pltpu.make_async_copy(packed, out, sem).wait()


def fourier(modes, field, table, devices, slots):
    band, lon_count, width = field.shape
    waves = table.shape[1]
    shape = (devices, 2, slots // 2, 2, band, width)
    return pl.pallas_call(
        fourier_kernel,
        grid=(band // FOURIER_LATS,),
        in_specs=[
            pl.BlockSpec(memory_space=pltpu.SMEM),
            pl.BlockSpec((FOURIER_LATS, lon_count, width), lambda i: (i, 0, 0)),
            pl.BlockSpec(table.shape, lambda i: (0, 0, 0)),
        ],
        out_specs=pl.BlockSpec(memory_space=pl.ANY),
        scratch_shapes=[pltpu.VMEM((waves * SPACING, width), F32)] * 2
        + [pltpu.VMEM(shape, BF16), pltpu.SemaphoreType.DMA],
        out_shape=jax.ShapeDtypeStruct(shape, BF16),
        compiler_params=pltpu.CompilerParams(vmem_limit_bytes=56 * 2**20),
        cost_estimate=pl.CostEstimate(
            flops=4 * band * lon_count * waves * width,
            bytes_accessed=2 * (band * lon_count * width + 4 * waves * band * width),
            transcendentals=0,
        ),
        name="fourier",
    )(modes, field, table)


def inverse_kernel(modes, pieces, table, out, even, odd):
    step = pl.program_id(0)
    lats, lon_count, width = out.shape
    half = lon_count // 2
    waves = table.shape[2]
    devices, _, pairs, _, band, _ = pieces.shape
    wide = (even, odd)

    def unpack(device, pair, parity, row):
        for p in range(2):
            start = pl.multiple_of((2 * row + p) * SPACING, 8)
            wide[parity][pl.ds(start, band), :] = pieces[device, parity, pair, p].astype(F32)

    @pl.when(step == 0)
    def _():
        for_each_tile(modes, devices, 2 * pairs, unpack)

    sums = []
    for parity in range(2):
        columns = [
            wide[parity][pl.ds(step * lats + a, waves, stride=SPACING), :].astype(BF16)
            for a in range(lats)
        ]
        sums.append(
            jnp.dot(table[parity], jnp.concatenate(columns, axis=1), preferred_element_type=F32)
        )
    low = (sums[0] + sums[1]).astype(BF16)
    high = (sums[0] - sums[1]).astype(BF16)
    for a in range(lats):
        out[a, :half, :] = low[:, a * width : (a + 1) * width]
        out[a, half:, :] = high[:, a * width : (a + 1) * width]


def inverse(modes, pieces, table):
    band, width = pieces.shape[-2:]
    _, half, waves = table.shape
    return pl.pallas_call(
        inverse_kernel,
        grid_spec=pltpu.PrefetchScalarGridSpec(
            num_scalar_prefetch=1,
            grid=(band // LATS,),
            in_specs=[
                pl.BlockSpec(memory_space=pltpu.VMEM),
                pl.BlockSpec(table.shape, lambda i, m: (0, 0, 0)),
            ],
            out_specs=pl.BlockSpec((LATS, 2 * half, width), lambda i, m: (i, 0, 0)),
            scratch_shapes=[pltpu.VMEM((waves * SPACING, width), F32)] * 2,
        ),
        out_shape=jax.ShapeDtypeStruct((band, 2 * half, width), BF16),
        compiler_params=pltpu.CompilerParams(vmem_limit_bytes=48 * 2**20),
        name="inverse_fourier",
    )(modes, pieces, table)


def carry_kernel(mixer, gain, out):
    core = lax.axis_index("lat") & 1
    rows, width = mixer.shape[1], gain.shape[1]
    out[:rows, :] = mixer[core]
    blocks = out.shape[1] // width
    deep = gain.shape[0] // 2 // blocks
    for block in range(blocks):
        start = pl.multiple_of(core * (gain.shape[0] // 2) + block * deep, deep)
        out[rows:, block * width : (block + 1) * width] = gain[pl.ds(start, deep), :]


def carry(mixer, gain):
    rows = mixer.shape[1] + gain.size // 2 // mixer.shape[2]
    return pl.pallas_call(
        carry_kernel,
        in_specs=[pl.BlockSpec(memory_space=pltpu.VMEM)] * 2,
        out_specs=pl.BlockSpec(memory_space=pltpu.VMEM),
        out_shape=jax.ShapeDtypeStruct((rows, mixer.shape[2]), BF16),
        name="carry",
    )(mixer, gain)


def gather_kernel(mixer, gain, *rest):
    mix, gains = rest[-2:]
    width = gain.shape[1]
    chan_parts = gains.shape[0]
    channels = chan_parts * width
    core = lax.axis_index("lat") & 1
    shares = rest[: chan_parts - 1], rest[chan_parts - 1 : 2 * (chan_parts - 1)]

    def place_mixer(hops, real, imag):
        here, below = hops * width, channels + hops * width
        if real is not None:
            mix[here : here + width, :] = real
        if imag is not None:
            mix[below : below + width, :] = imag

    place_mixer(0, mixer[0], mixer[1])
    gains[0] = gain[...]
    for hops in range(1, chan_parts):
        for swap in range(2):
            share = shares[swap][hops - 1]
            deep = share.shape[0] - width
            for block in range(chan_parts):
                start = pl.multiple_of((core ^ swap) * (gain.shape[0] // 2) + block * deep, deep)
                gains[hops, pl.ds(start, deep), :] = share[
                    width:, block * width : (block + 1) * width
                ]

            @pl.when(core ^ swap == 0)
            def _():
                place_mixer(hops, share[:width, :], None)

            @pl.when(core ^ swap == 1)
            def _():
                place_mixer(hops, None, share[:width, :])


def gather(mixer, gain, shares, chan_parts):
    channels2 = 2 * mixer.shape[2]
    whole = pl.BlockSpec(memory_space=pltpu.VMEM)
    return pl.pallas_call(
        gather_kernel,
        in_specs=[whole] * (2 + len(shares)),
        out_specs=[whole] * 2,
        out_shape=[
            jax.ShapeDtypeStruct((channels2, channels2 // 2), BF16),
            jax.ShapeDtypeStruct((chan_parts,) + gain.shape, BF16),
        ],
        compiler_params=pltpu.CompilerParams(vmem_limit_bytes=16 * 2**20),
        name="gather",
    )(mixer, gain, *shares)


def prepare_kernel(modes, place, basis_low, basis_high, kept):
    row, chan = place[0], place[1]
    pairs = pl.num_programs(0)
    degrees, lat_count = basis_low.shape[1:]
    block = degrees // 4
    begin_mode = chan * 2 * pairs + 2 * pl.program_id(0)
    lower = jnp.minimum(modes[begin_mode, row], modes[begin_mode + 1, row])
    higher = jnp.maximum(modes[begin_mode, row], modes[begin_mode + 1, row])

    def masked(basis, begin, count, wave):
        keep = begin + lax.broadcasted_iota(jnp.int32, (count, lat_count), 0) >= wave
        first = begin - (degrees - basis.shape[1])
        return jnp.where(keep, basis[0, first : first + count, :], jnp.zeros((), BF16))

    kept[0, :degrees, :] = masked(basis_low, 0, degrees, lower)
    kept[0, degrees : degrees + block, :] = masked(basis_high, degrees - block, block, higher)
    kept[0, degrees + block :, :] = masked(basis_high, degrees - 2 * block, block, higher)


def prepare(modes, place, basis, pairs):
    degrees, lat_count = basis.shape[1:]

    def basis_slot(which, pair, modes, place):
        begin = place[1] * 2 * pairs + 2 * pair
        swapped = (modes[begin, place[0]] > modes[begin + 1, place[0]]).astype(jnp.int32)
        return begin + (swapped if which == 0 else 1 - swapped)

    low, high = (1, degrees, lat_count), (1, degrees // 2, lat_count)
    return pl.pallas_call(
        prepare_kernel,
        grid_spec=pltpu.PrefetchScalarGridSpec(
            num_scalar_prefetch=2,
            grid=(pairs,),
            in_specs=[
                pl.BlockSpec(low, lambda i, m, c: (basis_slot(0, i, m, c), 0, 0)),
                pl.BlockSpec(high, lambda i, m, c: (basis_slot(1, i, m, c), 1, 0)),
            ],
            out_specs=pl.BlockSpec(
                (1, degrees + degrees // 2, lat_count), lambda i, m, c: (i, 0, 0)
            ),
        ),
        out_shape=jax.ShapeDtypeStruct((pairs, degrees + degrees // 2, lat_count), BF16),
        compiler_params=pltpu.CompilerParams(vmem_limit_bytes=16 * 2**20),
        name="prepare",
    )(modes, place, basis, basis)


def spectral_kernel(
    modes, place, pieces, kept_block, mix, gains, out, for_real, for_imag, mixed
):
    pair = pl.program_id(0)
    pairs = pl.num_programs(0)
    lat_parts, chan_parts, _, _, _, band, width = pieces.shape
    lat_count = lat_parts * band
    channels = chan_parts * width
    degrees = gains.shape[1]
    kept_low = kept_block.at[0, pl.ds(0, degrees)]
    kept_high = kept_block.at[0, pl.ds(degrees, degrees // 2)]
    block = degrees // 4
    row, chan = place[0], place[1]
    from_chan = [(chan + chan_parts - hops) % chan_parts for hops in range(chan_parts)]

    begin_mode = chan * 2 * pairs + 2 * pair
    lower = jnp.minimum(modes[begin_mode, row], modes[begin_mode + 1, row])
    higher = jnp.maximum(modes[begin_mode, row], modes[begin_mode + 1, row])

    def analyse(wave, kept, begin, count, target, spans):
        for p in range(2):
            for first_hop in range(0, chan_parts, 2):
                columns = [
                    pieces[:, from_chan[first_hop + k], wave & 1, 0, p].reshape(lat_count, width)
                    for k in range(2)
                ]
                part = jnp.dot(
                    kept[begin : begin + count, :],
                    jnp.concatenate(columns, axis=1),
                    preferred_element_type=F32,
                )
                for k in range(2):
                    hops = first_hop + k
                    for offset, rows, degree in spans:
                        factor = gains[hops, degree : degree + rows, :].astype(F32)
                        value = (
                            part[offset : offset + rows, k * width : (k + 1) * width] * factor
                        ).astype(BF16)
                        where = slice(target + offset, target + offset + rows)
                        first = slice(hops * width, (hops + 1) * width)
                        second = slice(channels + hops * width, channels + (hops + 1) * width)
                        for_real[where, first if p == 0 else second] = value if p == 0 else -value
                        for_imag[where, second if p == 0 else first] = value

    wide_low = lower < block

    @pl.when(wide_low)
    def _():
        analyse(lower, kept_low, 0, degrees, 0, [(0, degrees, 0)])
        mixed[degrees + block :, :] = jnp.zeros((block, 2 * channels), BF16)

    @pl.when(jnp.logical_not(wide_low))
    def _():
        analyse(lower, kept_low, block, degrees - block, block, [(0, degrees - block, block)])
        mixed[:block, :] = jnp.zeros((block, 2 * channels), BF16)


    @pl.when(wide_low)
    def _():
        analyse(higher, kept_high, 0, block, degrees, [(0, block, degrees - block)])

    @pl.when(jnp.logical_not(wide_low))
    def _():
        analyse(
            higher,
            kept_high,
            0,
            2 * block,
            degrees,
            [(0, block, degrees - block), (block, block, degrees - 2 * block)],
        )

    rows = pl.ds(pl.multiple_of(jnp.where(wide_low, 0, block), block), degrees + block)
    for p in range(2):
        columns = slice(p * channels, (p + 1) * channels)
        hidden = for_imag if p else for_real
        mixed[rows, columns] = jnp.dot(
            hidden[rows, :], mix[...], preferred_element_type=F32
        ).astype(BF16)

    for wave, kept, begin in ((lower, kept_low, 0), (higher, kept_high, degrees)):
        for p in range(2):
            for j in range(0, chan_parts, 2):
                start = p * channels + j * width
                back = lax.dot_general(
                    kept[...],
                    mixed[begin : begin + kept.shape[0], start : start + 2 * width],
                    (((0,), (0,)), ((), ())),
                    preferred_element_type=F32,
                ).astype(BF16)
                for k in range(2):
                    out[:, j + k, wave & 1, pair, p] = back[:, k * width : (k + 1) * width].reshape(
                        lat_parts, band, width
                    )


def spectral(modes, place, pieces, kept, mix, gains):
    pairs, rows, lat_count = kept.shape
    whole = pl.BlockSpec(memory_space=pltpu.VMEM)
    scalars = pl.BlockSpec(memory_space=pltpu.SMEM)
    one_pair = pl.BlockSpec(
        pieces.shape[:3] + (1,) + pieces.shape[4:], lambda i: (0, 0, 0, i, 0, 0, 0)
    )
    return pl.pallas_call(
        spectral_kernel,
        grid=(pairs,),
        in_specs=[
            scalars,
            scalars,
            one_pair,
            pl.BlockSpec((1, rows, lat_count), lambda i: (i, 0, 0)),
            whole,
            whole,
        ],
        out_specs=whole,
        scratch_shapes=[
            pltpu.VMEM((rows, mix.shape[0]), BF16),
            pltpu.VMEM((rows, mix.shape[0]), BF16),
            pltpu.VMEM((rows, mix.shape[0]), BF16),
        ],
        out_shape=jax.ShapeDtypeStruct(pieces.shape, BF16),
        compiler_params=pltpu.CompilerParams(vmem_limit_bytes=40 * 2**20),
        name="spectral",
    )(modes, place, pieces, kept, mix, gains)


def local(lat_parts, chan_parts, grid_field, mode_lists, lat_basis, degree_gain, channel_mixer):
    devices = lat_parts * chan_parts
    slots = lat_basis.shape[0] // chan_parts
    forward_table, back_table = folded_tables(grid_field.shape[1], mode_lists.size)
    forward_table = jnp.asarray(forward_table)
    modes = mode_lists.T
    lat_index = lax.axis_index("lat")
    place = jnp.stack([lat_index, lax.axis_index("chan")]).astype(jnp.int32)

    share = carry(channel_mixer, degree_gain)
    shares = [
        lax.ppermute(share, "chan", [(i, (i + hops) % chan_parts) for i in range(chan_parts)])
        for hops in range(1, chan_parts)
    ]
    sent = fourier(modes, grid_field, forward_table, devices, slots)
    sent, shares = lax.optimization_barrier((sent, shares))
    swapped = [lax.ppermute(s, "lat", [(i, i ^ 1) for i in range(lat_parts)]) for s in shares]
    got = lax.all_to_all(sent, ("lat", "chan"), 0, 0, tiled=True)
    got = got.reshape((lat_parts, chan_parts) + got.shape[1:])
    mix, gains = gather(channel_mixer, degree_gain, shares + swapped, chan_parts)
    late_modes, late_place, _ = lax.optimization_barrier((modes, place, swapped))
    kept = prepare(late_modes, late_place, lat_basis, slots // 2)
    back = spectral(late_modes, late_place, got, kept, mix, gains)
    back = back.reshape((devices,) + back.shape[2:])
    returned = lax.all_to_all(back, ("lat", "chan"), 0, 0, tiled=True)
    return inverse(modes, returned, jnp.asarray(back_table))


def solution(mesh):
    return jax.shard_map(
        functools.partial(local, mesh.shape["lat"], mesh.shape["chan"]),
        mesh=mesh,
        in_specs=(
            P("lat", None, "chan"),
            P(),
            P("lat", None, None),
            P(None, "chan"),
            P(None, "chan", None),
        ),
        out_specs=P("lat", None, "chan"),
        check_vma=False,
    )
```

```python
import functools
import math

import jax
import jax.numpy as jnp
import ml_dtypes
import numpy as np
from jax import lax
from jax.experimental import pallas as pl
from jax.experimental.pallas import tpu as pltpu
from jax.sharding import PartitionSpec as P

BF16 = jnp.bfloat16
F32 = jnp.float32
FOURIER_LATS = 8
LATS = 4
SPACING = 24


def folded_tables(lon_count, wave_count):
    half = lon_count // 2
    waves = np.arange(wave_count).reshape(-1, 2).T
    phases = (waves[:, :, None] * np.arange(half)[None, None, :]) % lon_count
    angles = phases * (2.0 * math.pi / lon_count)
    factor = 1.0 / math.sqrt(lon_count)
    table = np.stack([np.cos(angles) * factor, -np.sin(angles) * factor], axis=2)
    table = table.reshape(2, wave_count, half).astype(np.float32).astype(ml_dtypes.bfloat16)
    return table, np.ascontiguousarray(table.transpose(0, 2, 1))


def for_each_tile(modes, devices, slots, move, after=None):
    per_row = modes.shape[0] // slots
    last = modes.shape[0] * modes.shape[1] - 1

    def row_step(row, carry):
        for pair in range(modes.shape[0] // 2):
            mode = modes[2 * pair, row]
            even_row = jnp.where(mode & 1 == 1, last - mode, mode) >> 1
            device = row * per_row + 2 * pair // slots
            place = 2 * pair % slots // 2
            move(device, place, 0, even_row)
            move(device, place, 1, (last >> 1) - even_row)
        if after is not None:
            after(pl.ds(pl.multiple_of(row * per_row, per_row), per_row))
        return carry

    lax.fori_loop(0, devices // per_row, row_step, 0)


def fourier_kernel(modes, field, table, out, even, odd, packed, sem):
    step = pl.program_id(0)
    lats, lon_count, width = field.shape
    half = lon_count // 2
    waves = table.shape[1]
    devices, _, pairs, _, band, _ = out.shape
    wide = (even, odd)
    low = jnp.concatenate([field[a, :half, :] for a in range(lats)], axis=1)
    high = jnp.concatenate([field[a, half:, :] for a in range(lats)], axis=1)
    for parity in range(2):
        folded = low + high if parity == 0 else low - high
        result = jnp.dot(table[parity], folded, preferred_element_type=F32)
        for a in range(lats):
            rows = pl.ds(step * lats + a, waves, stride=SPACING)
            wide[parity][rows, :] = result[:, a * width : (a + 1) * width]

    def pack(device, pair, parity, row):
        for p in range(2):
            start = pl.multiple_of((2 * row + p) * SPACING, 8)
            packed[device, parity, pair, p] = wide[parity][pl.ds(start, band), :].astype(BF16)

    def send(some):
        pltpu.make_async_copy(packed.at[some], out.at[some], sem).start()

    @pl.when(step == pl.num_programs(0) - 1)
    def _():
        for_each_tile(modes, devices, 2 * pairs, pack, send)
        pltpu.make_async_copy(packed, out, sem).wait()


def fourier(modes, field, table, devices, slots):
    band, lon_count, width = field.shape
    waves = table.shape[1]
    shape = (devices, 2, slots // 2, 2, band, width)
    return pl.pallas_call(
        fourier_kernel,
        grid=(band // FOURIER_LATS,),
        in_specs=[
            pl.BlockSpec(memory_space=pltpu.SMEM),
            pl.BlockSpec((FOURIER_LATS, lon_count, width), lambda i: (i, 0, 0)),
            pl.BlockSpec(table.shape, lambda i: (0, 0, 0)),
        ],
        out_specs=pl.BlockSpec(memory_space=pl.ANY),
        scratch_shapes=[pltpu.VMEM((waves * SPACING, width), F32)] * 2
        + [pltpu.VMEM(shape, BF16), pltpu.SemaphoreType.DMA],
        out_shape=jax.ShapeDtypeStruct(shape, BF16),
        compiler_params=pltpu.CompilerParams(vmem_limit_bytes=56 * 2**20),
        cost_estimate=pl.CostEstimate(
            flops=4 * band * lon_count * waves * width,
            bytes_accessed=2 * (band * lon_count * width + 4 * waves * band * width),
            transcendentals=0,
        ),
        name="fourier",
    )(modes, field, table)


def inverse_kernel(modes, pieces, table, out, even, odd):
    step = pl.program_id(0)
    lats, lon_count, width = out.shape
    half = lon_count // 2
    waves = table.shape[2]
    devices, _, pairs, _, band, _ = pieces.shape
    wide = (even, odd)

    def unpack(device, pair, parity, row):
        for p in range(2):
            start = pl.multiple_of((2 * row + p) * SPACING, 8)
            wide[parity][pl.ds(start, band), :] = pieces[device, parity, pair, p].astype(F32)

    @pl.when(step == 0)
    def _():
        for_each_tile(modes, devices, 2 * pairs, unpack)

    sums = []
    for parity in range(2):
        columns = [
            wide[parity][pl.ds(step * lats + a, waves, stride=SPACING), :].astype(BF16)
            for a in range(lats)
        ]
        sums.append(
            jnp.dot(table[parity], jnp.concatenate(columns, axis=1), preferred_element_type=F32)
        )
    low = (sums[0] + sums[1]).astype(BF16)
    high = (sums[0] - sums[1]).astype(BF16)
    for a in range(lats):
        out[a, :half, :] = low[:, a * width : (a + 1) * width]
        out[a, half:, :] = high[:, a * width : (a + 1) * width]


def inverse(modes, pieces, table):
    band, width = pieces.shape[-2:]
    _, half, waves = table.shape
    return pl.pallas_call(
        inverse_kernel,
        grid_spec=pltpu.PrefetchScalarGridSpec(
            num_scalar_prefetch=1,
            grid=(band // LATS,),
            in_specs=[
                pl.BlockSpec(memory_space=pltpu.VMEM),
                pl.BlockSpec(table.shape, lambda i, m: (0, 0, 0)),
            ],
            out_specs=pl.BlockSpec((LATS, 2 * half, width), lambda i, m: (i, 0, 0)),
            scratch_shapes=[pltpu.VMEM((waves * SPACING, width), F32)] * 2,
        ),
        out_shape=jax.ShapeDtypeStruct((band, 2 * half, width), BF16),
        compiler_params=pltpu.CompilerParams(vmem_limit_bytes=48 * 2**20),
        name="inverse_fourier",
    )(modes, pieces, table)


def hop_order(chan_parts):
    return sorted(range(1, chan_parts), key=lambda hops: min(hops, chan_parts - hops))


def carry_kernel(mixer, gain, out):
    core = lax.axis_index("lat") & 1
    rows, width = mixer.shape[1], gain.shape[1]
    out[:rows, :] = mixer[core]
    blocks = out.shape[1] // width
    deep = gain.shape[0] // 2 // blocks
    for block in range(blocks):
        start = pl.multiple_of(core * (gain.shape[0] // 2) + block * deep, deep)
        out[rows:, block * width : (block + 1) * width] = gain[pl.ds(start, deep), :]


def carry(mixer, gain):
    rows = mixer.shape[1] + gain.size // 2 // mixer.shape[2]
    return pl.pallas_call(
        carry_kernel,
        in_specs=[pl.BlockSpec(memory_space=pltpu.VMEM)] * 2,
        out_specs=pl.BlockSpec(memory_space=pltpu.VMEM),
        out_shape=jax.ShapeDtypeStruct((rows, mixer.shape[2]), BF16),
        name="carry",
    )(mixer, gain)


def gather_kernel(mixer, gain, *rest):
    mix, gains = rest[-2:]
    width = gain.shape[1]
    chan_parts = gains.shape[0]
    channels = chan_parts * width
    core = lax.axis_index("lat") & 1
    shares = rest[: chan_parts - 1], rest[chan_parts - 1 : 2 * (chan_parts - 1)]

    def place_mixer(hops, real, imag):
        here, below = hops * width, channels + hops * width
        if real is not None:
            mix[here : here + width, :] = real
        if imag is not None:
            mix[below : below + width, :] = imag

    place_mixer(0, mixer[0], mixer[1])
    gains[0] = gain[...]
    for index, hops in enumerate(hop_order(chan_parts)):
        for swap in range(2):
            share = shares[swap][index]
            deep = share.shape[0] - width
            for block in range(chan_parts):
                start = pl.multiple_of((core ^ swap) * (gain.shape[0] // 2) + block * deep, deep)
                gains[hops, pl.ds(start, deep), :] = share[
                    width:, block * width : (block + 1) * width
                ]

            @pl.when(core ^ swap == 0)
            def _():
                place_mixer(hops, share[:width, :], None)

            @pl.when(core ^ swap == 1)
            def _():
                place_mixer(hops, None, share[:width, :])


def gather(mixer, gain, shares, chan_parts):
    channels2 = 2 * mixer.shape[2]
    whole = pl.BlockSpec(memory_space=pltpu.VMEM)
    return pl.pallas_call(
        gather_kernel,
        in_specs=[whole] * (2 + len(shares)),
        out_specs=[whole] * 2,
        out_shape=[
            jax.ShapeDtypeStruct((channels2, channels2 // 2), BF16),
            jax.ShapeDtypeStruct((chan_parts,) + gain.shape, BF16),
        ],
        compiler_params=pltpu.CompilerParams(vmem_limit_bytes=16 * 2**20),
        name="gather",
    )(mixer, gain, *shares)


def prepare_kernel(modes, place, basis_low, basis_high, kept):
    row, chan = place[0], place[1]
    pairs = pl.num_programs(0)
    degrees, lat_count = basis_low.shape[1:]
    block = degrees // 4
    begin_mode = chan * 2 * pairs + 2 * pl.program_id(0)
    lower = jnp.minimum(modes[begin_mode, row], modes[begin_mode + 1, row])
    higher = jnp.maximum(modes[begin_mode, row], modes[begin_mode + 1, row])

    def masked(basis, begin, count, wave):
        keep = begin + lax.broadcasted_iota(jnp.int32, (count, lat_count), 0) >= wave
        first = begin - (degrees - basis.shape[1])
        return jnp.where(keep, basis[0, first : first + count, :], jnp.zeros((), BF16))

    kept[0, :degrees, :] = masked(basis_low, 0, degrees, lower)
    kept[0, degrees : degrees + block, :] = masked(basis_high, degrees - block, block, higher)
    kept[0, degrees + block :, :] = masked(basis_high, degrees - 2 * block, block, higher)


def prepare(modes, place, basis, pairs):
    degrees, lat_count = basis.shape[1:]

    def basis_slot(which, pair, modes, place):
        begin = place[1] * 2 * pairs + 2 * pair
        swapped = (modes[begin, place[0]] > modes[begin + 1, place[0]]).astype(jnp.int32)
        return begin + (swapped if which == 0 else 1 - swapped)

    low, high = (1, degrees, lat_count), (1, degrees // 2, lat_count)
    return pl.pallas_call(
        prepare_kernel,
        grid_spec=pltpu.PrefetchScalarGridSpec(
            num_scalar_prefetch=2,
            grid=(pairs,),
            in_specs=[
                pl.BlockSpec(low, lambda i, m, c: (basis_slot(0, i, m, c), 0, 0)),
                pl.BlockSpec(high, lambda i, m, c: (basis_slot(1, i, m, c), 1, 0)),
            ],
            out_specs=pl.BlockSpec(
                (1, degrees + degrees // 2, lat_count), lambda i, m, c: (i, 0, 0)
            ),
        ),
        out_shape=jax.ShapeDtypeStruct((pairs, degrees + degrees // 2, lat_count), BF16),
        compiler_params=pltpu.CompilerParams(vmem_limit_bytes=16 * 2**20),
        name="prepare",
    )(modes, place, basis, basis)


def spectral_kernel(
    modes, place, pieces, kept_block, mix, gains, out, for_real, for_imag, mixed
):
    pair = pl.program_id(0)
    pairs = pl.num_programs(0)
    lat_parts, chan_parts, _, _, _, band, width = pieces.shape
    lat_count = lat_parts * band
    channels = chan_parts * width
    degrees = gains.shape[1]
    kept_low = kept_block.at[0, pl.ds(0, degrees)]
    kept_high = kept_block.at[0, pl.ds(degrees, degrees // 2)]
    block = degrees // 4
    row, chan = place[0], place[1]
    from_chan = [(chan + chan_parts - hops) % chan_parts for hops in range(chan_parts)]

    begin_mode = chan * 2 * pairs + 2 * pair
    lower = jnp.minimum(modes[begin_mode, row], modes[begin_mode + 1, row])
    higher = jnp.maximum(modes[begin_mode, row], modes[begin_mode + 1, row])

    def analyse(wave, kept, begin, count, target, spans):
        for p in range(2):
            for first_hop in range(0, chan_parts, 2):
                columns = [
                    pieces[:, from_chan[first_hop + k], wave & 1, 0, p].reshape(lat_count, width)
                    for k in range(2)
                ]
                part = jnp.dot(
                    kept[begin : begin + count, :],
                    jnp.concatenate(columns, axis=1),
                    preferred_element_type=F32,
                )
                for k in range(2):
                    hops = first_hop + k
                    for offset, rows, degree in spans:
                        factor = gains[hops, degree : degree + rows, :].astype(F32)
                        value = (
                            part[offset : offset + rows, k * width : (k + 1) * width] * factor
                        ).astype(BF16)
                        where = slice(target + offset, target + offset + rows)
                        first = slice(hops * width, (hops + 1) * width)
                        second = slice(channels + hops * width, channels + (hops + 1) * width)
                        for_real[where, first if p == 0 else second] = value if p == 0 else -value
                        for_imag[where, second if p == 0 else first] = value

    wide_low = lower < block

    @pl.when(wide_low)
    def _():
        analyse(lower, kept_low, 0, degrees, 0, [(0, degrees, 0)])
        mixed[degrees + block :, :] = jnp.zeros((block, 2 * channels), BF16)

    @pl.when(jnp.logical_not(wide_low))
    def _():
        analyse(lower, kept_low, block, degrees - block, block, [(0, degrees - block, block)])
        mixed[:block, :] = jnp.zeros((block, 2 * channels), BF16)


    @pl.when(wide_low)
    def _():
        analyse(higher, kept_high, 0, block, degrees, [(0, block, degrees - block)])

    @pl.when(jnp.logical_not(wide_low))
    def _():
        analyse(
            higher,
            kept_high,
            0,
            2 * block,
            degrees,
            [(0, block, degrees - block), (block, block, degrees - 2 * block)],
        )

    rows = pl.ds(pl.multiple_of(jnp.where(wide_low, 0, block), block), degrees + block)
    for p in range(2):
        columns = slice(p * channels, (p + 1) * channels)
        hidden = for_imag if p else for_real
        mixed[rows, columns] = jnp.dot(
            hidden[rows, :], mix[...], preferred_element_type=F32
        ).astype(BF16)

    for wave, kept, begin in ((lower, kept_low, 0), (higher, kept_high, degrees)):
        for p in range(2):
            for j in range(0, chan_parts, 2):
                start = p * channels + j * width
                back = lax.dot_general(
                    kept[...],
                    mixed[begin : begin + kept.shape[0], start : start + 2 * width],
                    (((0,), (0,)), ((), ())),
                    preferred_element_type=F32,
                ).astype(BF16)
                for k in range(2):
                    out[:, j + k, wave & 1, pair, p] = back[:, k * width : (k + 1) * width].reshape(
                        lat_parts, band, width
                    )


def spectral(modes, place, pieces, kept, mix, gains):
    pairs, rows, lat_count = kept.shape
    whole = pl.BlockSpec(memory_space=pltpu.VMEM)
    scalars = pl.BlockSpec(memory_space=pltpu.SMEM)
    one_pair = pl.BlockSpec(
        pieces.shape[:3] + (1,) + pieces.shape[4:], lambda i: (0, 0, 0, i, 0, 0, 0)
    )
    return pl.pallas_call(
        spectral_kernel,
        grid=(pairs,),
        in_specs=[
            scalars,
            scalars,
            one_pair,
            pl.BlockSpec((1, rows, lat_count), lambda i: (i, 0, 0)),
            whole,
            whole,
        ],
        out_specs=whole,
        scratch_shapes=[
            pltpu.VMEM((rows, mix.shape[0]), BF16),
            pltpu.VMEM((rows, mix.shape[0]), BF16),
            pltpu.VMEM((rows, mix.shape[0]), BF16),
        ],
        out_shape=jax.ShapeDtypeStruct(pieces.shape, BF16),
        compiler_params=pltpu.CompilerParams(vmem_limit_bytes=40 * 2**20),
        name="spectral",
    )(modes, place, pieces, kept, mix, gains)


def local(lat_parts, chan_parts, grid_field, mode_lists, lat_basis, degree_gain, channel_mixer):
    devices = lat_parts * chan_parts
    slots = lat_basis.shape[0] // chan_parts
    forward_table, back_table = folded_tables(grid_field.shape[1], mode_lists.size)
    forward_table = jnp.asarray(forward_table)
    modes = mode_lists.T
    lat_index = lax.axis_index("lat")
    place = jnp.stack([lat_index, lax.axis_index("chan")]).astype(jnp.int32)

    share = carry(channel_mixer, degree_gain)
    shares = [
        lax.ppermute(share, "chan", [(i, (i + hops) % chan_parts) for i in range(chan_parts)])
        for hops in hop_order(chan_parts)
    ]
    sent = fourier(modes, grid_field, forward_table, devices, slots)
    sent, shares = lax.optimization_barrier((sent, shares))
    swapped = [lax.ppermute(s, "lat", [(i, i ^ 1) for i in range(lat_parts)]) for s in shares]
    got = lax.all_to_all(sent, ("lat", "chan"), 0, 0, tiled=True)
    got = got.reshape((lat_parts, chan_parts) + got.shape[1:])
    mix, gains = gather(channel_mixer, degree_gain, shares + swapped, chan_parts)
    late_modes, late_place, _ = lax.optimization_barrier((modes, place, swapped))
    kept = prepare(late_modes, late_place, lat_basis, slots // 2)
    back = spectral(late_modes, late_place, got, kept, mix, gains)
    back = back.reshape((devices,) + back.shape[2:])
    returned = lax.all_to_all(back, ("lat", "chan"), 0, 0, tiled=True)
    return inverse(modes, returned, jnp.asarray(back_table))


def solution(mesh):
    return jax.shard_map(
        functools.partial(local, mesh.shape["lat"], mesh.shape["chan"]),
        mesh=mesh,
        in_specs=(
            P("lat", None, "chan"),
            P(),
            P("lat", None, None),
            P(None, "chan"),
            P(None, "chan", None),
        ),
        out_specs=P("lat", None, "chan"),
        check_vma=False,
    )
```
